32 devices in a mesh: cell: 16 (over z, y, x), view: 2 (over core).
Axes of the slice: x: 2, y: 2, z: 4, core: 2. Of those that a mesh axis runs over, the one named last changes fastest.
Arguments:
- gauss_params: float32 [59, 614400], P(None, ('cell', 'view')), as said below
- visible: int32 [4, 614400], P(None, ('cell', 'view')), may hold values 0 or 1
- cameras: float32 [4, 15], replicated, as said below
- tile_ids: int32 [16, 2, 120], P('cell', 'view'), may hold values from 0 to 1919, as said below
- tile_blocks: int32 [16, 2, 120, 2], P('cell', 'view'), may hold values from -1 to 4799, as said below
- target: float32 [2, 3, 256, 1920], P('view', None, 'cell'), as said below
Outputs:
- image: float32 [2, 3, 256, 1920], P('view', None, 'cell')
- loss_map: float32 [2, 256, 1920], P('view', 'cell')
The draws below stay inside these ranges and needn't reach their ends.
Inputs may be any that keep to these rules, and one draw needn't show every extreme that they name: `tile_ids`: for each view index v the lists of the 16 renderers (c, v) together name each of the 1920 tiles of views 2 v and 2 v + 1 exactly once. The tiles of one renderer lie in 120 different columns t % 120, at most 8 of them in one stripe t // 120, and some renderer reaches 8. `tile_blocks`: an entry names a block g (Gaussians 128 g to 128 g + 127, held by device g // 150 of cell+view) or is -1. The live entries of a tile come first, 1 to 2 of them, and some tile has 2. Every block is named by exactly one tile of all. The live entries of one renderer number exactly 150; at most 5 of them name blocks of one device, and every renderer reaches 5 with some device. `gauss_params`: rows 0 to 2: mean; 3 to 5: logarithms of the scales; 6 to 9: rotation quaternion, real part in row 6 between 1 and 2; row 10: opacity logit, at most 2; row 11 + 3 j + k: coefficient j of the spherical harmonics of colour channel k. Every Gaussian of a block named by a tile lies at depth about 4 to 40 in front of the camera of that tile's view. `cameras`: row w: a rotation (world to camera, row-major) in entries 0 to 8, the translation in 9 to 11, the focal length in pixels in 12 and the principal point (column, row) in 13 and 14. `target`: every value lies between 0.02 and 1.
All inputs are finite; a program needn't handle non-finite values. No bound on the sum of `visible` on one device may be relied on, other than what follows from the above.
Results may differ from the reference program's by a relative error of at most 0.0003.
Values sent between devices are 32-bit elements; how exact they have to be, the bound alone decides.
No kernel may reach another device: no remote copies, remote signals or barrier semaphores. Data moves between devices by JAX's collectives and lax.ppermute only.
A program may use at most 64 MiB of HBM per device.

```python
import math
import jax
import jax.numpy as jnp
from jax import lax

GBLK = 128
FEAT = 59
IMG_W = 1920
BLK_DEV = 150
TILE_DEV = 120
LIST = 2
VIEWS = 4
IMG_H = 128
ROWS = 256
GAUSS = 614400
CAP = 5
RCAP = 8
N_CELL = 16
N_VIEW = 2


def chain(left, right):
    return [[left[line][0] * right[0][column] + left[line][1] * right[1][column] + left[line][2] * right[2][column] for column in range(3)] for line in range(3)]


def camera_table(key):
    keys = jax.random.split(jax.random.fold_in(key, 101), 7)
    yaw = jax.random.uniform(keys[0], (VIEWS,), jnp.float32, -math.pi, math.pi)
    pitch = jax.random.uniform(keys[1], (VIEWS,), jnp.float32, -0.6, 0.6)
    roll = jax.random.uniform(keys[2], (VIEWS,), jnp.float32, -0.3, 0.3)
    offset = 30.0 * jax.random.normal(keys[3], (3, VIEWS), jnp.float32)
    focal_len = jax.random.uniform(keys[4], (VIEWS,), jnp.float32, 900.0, 1300.0)
    centre_col = 0.5 * IMG_W + jax.random.uniform(keys[5], (VIEWS,), jnp.float32, -30.0, 30.0)
    centre_row = 0.5 * IMG_H + jax.random.uniform(keys[6], (VIEWS,), jnp.float32, -30.0, 30.0)
    all_zero = jnp.zeros((VIEWS,), jnp.float32)
    all_one = jnp.ones((VIEWS,), jnp.float32)
    turn_y = [[jnp.cos(yaw), all_zero, jnp.sin(yaw)], [all_zero, all_one, all_zero], [-jnp.sin(yaw), all_zero, jnp.cos(yaw)]]
    turn_x = [[all_one, all_zero, all_zero], [all_zero, jnp.cos(pitch), -jnp.sin(pitch)], [all_zero, jnp.sin(pitch), jnp.cos(pitch)]]
    turn_z = [[jnp.cos(roll), -jnp.sin(roll), all_zero], [jnp.sin(roll), jnp.cos(roll), all_zero], [all_zero, all_zero, all_one]]
    rotation = chain(turn_z, chain(turn_x, turn_y))
    flat_rows = [rotation[line][column] for line in range(3) for column in range(3)]
    return jnp.stack(flat_rows + [offset[0], offset[1], offset[2], focal_len, centre_col, centre_row], axis=1)


def forced_pick(key, total, count, wanted):
    perm = jax.random.permutation(key, total).astype(jnp.int32)
    special = jnp.zeros((total,), jnp.int32)
    for value in wanted:
        special = special + (perm == value).astype(jnp.int32)
    scores = jnp.where(special > 0, -1, jnp.arange(total, dtype=jnp.int32))
    order = jnp.argsort(scores, stable=True)
    return perm[order][:count]


def layout(key):
    keys = jax.random.split(jax.random.fold_in(key, 202), 6)
    devices = N_CELL * N_VIEW
    half = N_CELL // 2
    quarter = N_CELL // 4
    stripe_wanted = [1, N_CELL // 2, N_CELL - 1]
    shifts = jax.vmap(lambda subkey: forced_pick(subkey, RCAP * N_CELL, TILE_DEV, stripe_wanted) % N_CELL)(jax.random.split(keys[0], N_VIEW))
    stripes = (jnp.arange(N_CELL, dtype=jnp.int32)[:, None, None] - shifts[None, :, :].astype(jnp.int32)) % N_CELL
    ordered = stripes * TILE_DEV + jnp.arange(TILE_DEV, dtype=jnp.int32)[None, None, :]
    shuffles = jax.vmap(lambda subkey: jax.random.permutation(subkey, TILE_DEV))(jax.random.split(keys[1], devices)).reshape(N_CELL, N_VIEW, TILE_DEV)
    tile_table = jnp.take_along_axis(ordered, shuffles, axis=2).astype(jnp.int32)
    owner_wanted = [1, devices // 2, devices - 1]
    spread_off = (forced_pick(keys[2], CAP * devices, BLK_DEV, owner_wanted) % devices).astype(jnp.int32)
    renderer = jnp.arange(devices, dtype=jnp.int32)[:, None]
    owners = (renderer - spread_off[None, :]) % devices
    block_gid = owners * BLK_DEV + jnp.arange(BLK_DEV, dtype=jnp.int32)[None, :]
    entry_order = jax.vmap(lambda subkey: jax.random.permutation(subkey, BLK_DEV))(jax.random.split(keys[3], devices))
    entry_gid = jnp.take_along_axis(block_gid, entry_order, axis=1)
    slot_total = TILE_DEV * (LIST - 1)
    scores = jax.vmap(lambda subkey: jax.random.permutation(subkey, slot_total))(jax.random.split(keys[4], devices)).astype(jnp.int32)
    full_tile = jax.random.randint(keys[5], (devices, 1), 0, TILE_DEV)
    scores = jnp.where((jnp.arange(slot_total, dtype=jnp.int32) // (LIST - 1))[None, :] == full_tile, -1, scores)
    ranking = jnp.argsort(jnp.argsort(scores, axis=1, stable=True), axis=1, stable=True)
    chosen = (ranking < BLK_DEV - TILE_DEV).astype(jnp.int32)
    counts = 1 + jnp.sum(chosen.reshape(devices, TILE_DEV, LIST - 1), axis=2)
    starts = jnp.cumsum(counts, axis=1) - counts
    depth_pos = jnp.arange(LIST, dtype=jnp.int32)
    positions = starts[:, :, None] + depth_pos[None, None, :]
    is_live = depth_pos[None, None, :] < counts[:, :, None]
    picked = jnp.take_along_axis(entry_gid, jnp.minimum(positions, BLK_DEV - 1).reshape(devices, -1), axis=1).reshape(devices, TILE_DEV, LIST)
    list_table = jnp.where(is_live, picked, -1).astype(jnp.int32).reshape(N_CELL, N_VIEW, TILE_DEV, LIST)
    tile_flat = tile_table.reshape(devices, TILE_DEV)
    entry_pos = jnp.arange(BLK_DEV, dtype=jnp.int32)
    holder = jnp.sum((starts[:, None, :] <= entry_pos[None, :, None]).astype(jnp.int32), axis=2) - 1
    entry_tile = jnp.take_along_axis(tile_flat, holder, axis=1)
    group_of = (jnp.arange(devices, dtype=jnp.int32) % N_VIEW)[:, None]
    shifted = (entry_tile // TILE_DEV - quarter) % N_CELL
    entry_view = 2 * group_of + shifted // half
    entry_x = 16 * (entry_tile % TILE_DEV)
    entry_y = 16 * (shifted % half)
    flat_gid = entry_gid.reshape(-1)
    block_view = jnp.zeros((devices * BLK_DEV,), jnp.int32).at[flat_gid].set(entry_view.reshape(-1))
    block_x = jnp.zeros((devices * BLK_DEV,), jnp.int32).at[flat_gid].set(entry_x.reshape(-1))
    block_y = jnp.zeros((devices * BLK_DEV,), jnp.int32).at[flat_gid].set(entry_y.reshape(-1))
    return (tile_table, list_table, block_view, block_x, block_y)


def draw_cameras(key, part):
    table = camera_table(key)
    return table


def draw_tile_ids(key, part):
    tile_table, list_table, block_view, block_x, block_y = layout(key)
    return tile_table


def draw_tile_blocks(key, part):
    tile_table, list_table, block_view, block_x, block_y = layout(key)
    return list_table


def draw_gauss_params(key, part):
    table = camera_table(key)
    tile_table, list_table, block_view, block_x, block_y = layout(key)
    key = jax.random.fold_in(key, 3)
    keys = jax.random.split(key, 9)
    count = GAUSS
    view_of = jnp.repeat(block_view, GBLK)
    per_gauss = [table[:, number][view_of] for number in range(15)]
    screen_x = jnp.repeat(block_x, GBLK).astype(jnp.float32) + jax.random.uniform(keys[0], (count,), jnp.float32, -3.0, 19.0)
    screen_y = jnp.repeat(block_y, GBLK).astype(jnp.float32) + jax.random.uniform(keys[1], (count,), jnp.float32, -3.0, 19.0)
    depths = jax.random.uniform(keys[2], (count,), jnp.float32, 4.0, 40.0)
    focal_len = per_gauss[12]
    in_camera = [(screen_x - per_gauss[13]) * depths / focal_len, (screen_y - per_gauss[14]) * depths / focal_len, depths]
    relative = [in_camera[line] - per_gauss[9 + line] for line in range(3)]
    world = [per_gauss[column] * relative[0] + per_gauss[3 + column] * relative[1] + per_gauss[6 + column] * relative[2] for column in range(3)]
    spread_px = jnp.exp(jax.random.uniform(keys[3], (count,), jnp.float32, 0.0, math.log(3.0)))
    log_size = jnp.log(spread_px * depths / focal_len)
    log_scales = log_size[None, :] + 0.25 * jax.random.normal(keys[4], (3, count), jnp.float32)
    real_part = jax.random.uniform(keys[5], (1, count), jnp.float32, 1.0, 2.0)
    imag_part = 0.6 * jax.random.normal(keys[6], (3, count), jnp.float32)
    logits = jax.random.uniform(keys[7], (1, count), jnp.float32, -6.0, 2.0)
    spread_sh = jnp.concatenate([jnp.full((3, 1), 0.8, jnp.float32), jnp.full((45, 1), 0.2, jnp.float32)], axis=0)
    harmonic = jax.random.normal(keys[8], (48, count), jnp.float32) * spread_sh
    return jnp.concatenate([jnp.stack(world), log_scales, real_part, imag_part, logits, harmonic], axis=0)


def draw_target(key, part):
    key = jax.random.fold_in(key, 7)
    keys = jax.random.split(key, 3)
    node_rows = ROWS // 16 + 1
    node_cols = IMG_W // 16 + 1
    base = jax.random.uniform(keys[0], (N_VIEW, 1, node_rows, node_cols), jnp.float32, 0.15, 0.7)
    tint = 0.06 * jax.random.normal(keys[1], (N_VIEW, 3, node_rows, node_cols), jnp.float32)
    grain = 0.03 * jax.random.normal(keys[2], (N_VIEW, 3, ROWS, IMG_W), jnp.float32)
    nodes = base + tint
    row_pos = jnp.arange(ROWS, dtype=jnp.int32)
    col_pos = jnp.arange(IMG_W, dtype=jnp.int32)
    row_low = row_pos // 16
    col_low = col_pos // 16
    row_frac = (row_pos % 16).astype(jnp.float32) / 16.0
    col_frac = (col_pos % 16).astype(jnp.float32) / 16.0
    top_rows = nodes[:, :, row_low, :]
    next_rows = nodes[:, :, row_low + 1, :]
    row_mixed = top_rows * (1.0 - row_frac)[:, None] + next_rows * row_frac[:, None]
    left_side = row_mixed[:, :, :, col_low]
    right_side = row_mixed[:, :, :, col_low + 1]
    smooth = left_side * (1.0 - col_frac) + right_side * col_frac
    return jnp.clip(smooth + grain, 0.02, 1.0)


def touch_ends(result, stream_key, smallest, largest):
    extent = result.shape
    index_at = [jax.random.randint(jax.random.fold_in(stream_key, axis), (), 0, extent[axis]) for axis in range(len(extent))]
    result = result.at[tuple(index_at)].set(smallest)
    longest = extent.index(max(extent))
    index_at[longest] = (index_at[longest] + 1) % extent[longest]
    return result.at[tuple(index_at)].set(largest)


def setup_inputs(seed: int = 0) -> dict:
    key_list = jax.random.split(jax.random.key(seed), 7)
    return {
        "gauss_params": draw_gauss_params(jax.random.fold_in(key_list[6], 71), 0),
        "visible": touch_ends((jax.random.randint(key_list[1], (VIEWS, GAUSS), 0, 8) < 7).astype(jnp.int32), jax.random.fold_in(key_list[1], 1), 0, 1),
        "cameras": draw_cameras(jax.random.fold_in(key_list[6], 71), 0),
        "tile_ids": draw_tile_ids(jax.random.fold_in(key_list[6], 71), 0),
        "tile_blocks": draw_tile_blocks(jax.random.fold_in(key_list[6], 71), 0),
        "target": draw_target(jax.random.fold_in(key_list[6], 71), 0),
    }


def harmonics(unit_x, unit_y, unit_z):
    square_x = unit_x * unit_x
    square_y = unit_y * unit_y
    square_z = unit_z * unit_z
    return [0.28209479177387814 + 0.0 * unit_x, -0.4886025119029199 * unit_y, 0.4886025119029199 * unit_z, -0.4886025119029199 * unit_x, 1.0925484305920792 * unit_x * unit_y, -1.0925484305920792 * unit_y * unit_z, 0.31539156525252005 * (2.0 * square_z - square_x - square_y), -1.0925484305920792 * unit_x * unit_z, 0.5462742152960396 * (square_x - square_y), -0.5900435899266435 * unit_y * (3.0 * square_x - square_y), 2.890611442640554 * unit_x * unit_y * unit_z, -0.4570457994644658 * unit_y * (4.0 * square_z - square_x - square_y), 0.3731763325901154 * unit_z * (2.0 * square_z - 3.0 * square_x - 3.0 * square_y), -0.4570457994644658 * unit_x * (4.0 * square_z - square_x - square_y), 1.445305721320277 * unit_z * (square_x - square_y), -0.5900435899266435 * unit_x * (square_x - 3.0 * square_y)]

def project(raw_params, camera, seen_mask):
    entries = [camera[:, number][:, None] for number in range(15)]
    rotation = [[entries[0], entries[1], entries[2]], [entries[3], entries[4], entries[5]], [entries[6], entries[7], entries[8]]]
    offset = [entries[9], entries[10], entries[11]]
    focal_len = entries[12]
    centre_pos = [raw_params[:, number] for number in range(3)]
    in_camera = [rotation[member][0] * centre_pos[0] + rotation[member][1] * centre_pos[1] + rotation[member][2] * centre_pos[2] + offset[member] for member in range(3)]
    depths = in_camera[2]
    screen_x = focal_len * in_camera[0] / depths + entries[13]
    screen_y = focal_len * in_camera[1] / depths + entries[14]
    quaternion = [raw_params[:, 6 + number] for number in range(4)]
    length = jnp.sqrt(quaternion[0] * quaternion[0] + quaternion[1] * quaternion[1] + quaternion[2] * quaternion[2] + quaternion[3] * quaternion[3])
    real_part, imag_x, imag_y, imag_z = [part / length for part in quaternion]
    turn_q = [[1.0 - 2.0 * (imag_y * imag_y + imag_z * imag_z), 2.0 * (imag_x * imag_y - real_part * imag_z), 2.0 * (imag_x * imag_z + real_part * imag_y)], [2.0 * (imag_x * imag_y + real_part * imag_z), 1.0 - 2.0 * (imag_x * imag_x + imag_z * imag_z), 2.0 * (imag_y * imag_z - real_part * imag_x)], [2.0 * (imag_x * imag_z - real_part * imag_y), 2.0 * (imag_y * imag_z + real_part * imag_x), 1.0 - 2.0 * (imag_x * imag_x + imag_y * imag_y)]]
    squares = [jnp.exp(2.0 * raw_params[:, 3 + number]) for number in range(3)]
    jacobian = [[focal_len / depths, 0.0 * depths, -focal_len * in_camera[0] / (depths * depths)], [0.0 * depths, focal_len / depths, -focal_len * in_camera[1] / (depths * depths)]]
    with_cam = [[jacobian[member][0] * rotation[0][column] + jacobian[member][1] * rotation[1][column] + jacobian[member][2] * rotation[2][column] for column in range(3)] for member in range(2)]
    whole = [[with_cam[member][0] * turn_q[0][column] + with_cam[member][1] * turn_q[1][column] + with_cam[member][2] * turn_q[2][column] for column in range(3)] for member in range(2)]
    cov_a = squares[0] * whole[0][0] * whole[0][0] + squares[1] * whole[0][1] * whole[0][1] + squares[2] * whole[0][2] * whole[0][2] + 0.3
    cov_b = squares[0] * whole[0][0] * whole[1][0] + squares[1] * whole[0][1] * whole[1][1] + squares[2] * whole[0][2] * whole[1][2]
    cov_c = squares[0] * whole[1][0] * whole[1][0] + squares[1] * whole[1][1] * whole[1][1] + squares[2] * whole[1][2] * whole[1][2] + 0.3
    determinant = cov_a * cov_c - cov_b * cov_b
    eye_pos = [-(rotation[0][column] * offset[0] + rotation[1][column] * offset[1] + rotation[2][column] * offset[2]) for column in range(3)]
    heading = [centre_pos[column] - eye_pos[column] for column in range(3)]
    distance = jnp.sqrt(heading[0] * heading[0] + heading[1] * heading[1] + heading[2] * heading[2])
    basis = harmonics(heading[0] / distance, heading[1] / distance, heading[2] / distance)
    colours = [jnp.maximum(0.5 + sum((basis[number] * raw_params[:, 11 + 3 * number + channel] for number in range(16))), 0.0) for channel in range(3)]
    opacity = seen_mask / (1.0 + jnp.exp(-raw_params[:, 10]))
    return jnp.stack([screen_x, screen_y, cov_c / determinant, -cov_b / determinant, cov_a / determinant, opacity] + colours, axis=1)

def composite(features, across_x, across_y, log_trans, colour):
    dist_x = across_x[:, :, None] - features[:, 0][:, None, :]
    dist_y = across_y[:, :, None] - features[:, 1][:, None, :]
    exponent = -0.5 * (features[:, 2][:, None, :] * dist_x * dist_x + features[:, 4][:, None, :] * dist_y * dist_y) - features[:, 3][:, None, :] * dist_x * dist_y
    alphas = features[:, 5][:, None, :] * jnp.exp(exponent)
    log_keep = jnp.log1p(-alphas)
    before = jnp.cumsum(log_keep, axis=2) - log_keep
    weights = alphas * jnp.exp(log_trans[:, :, None] + before)
    colour = colour + jnp.einsum('tpg,tcg->tcp', weights, features[:, 6:9], precision=lax.Precision.HIGHEST)
    return (log_trans + lax.optimization_barrier(jnp.sum(log_keep, axis=2)), colour)

def window_taps():
    offsets = jnp.arange(11).astype(jnp.float32) - 5.0
    taps = jnp.exp(-offsets * offsets / 4.5)
    return taps / jnp.sum(taps)

def blur(stack, row_count):
    taps = window_taps()
    columns = stack.shape[-1]
    widths = [(0, 0)] * (stack.ndim - 1) + [(5, 5)]
    wide = jnp.pad(stack, widths)
    across = sum((taps[number] * wide[..., number:number + columns] for number in range(11)))
    return sum((taps[number] * across[..., number:number + row_count, :] for number in range(11)))

def stripe_loss(images, targets, row_count):
    stack = jnp.stack([images, targets, images * images, targets * targets, images * targets])
    blurred = blur(stack, row_count)
    mean_x = blurred[0]
    mean_y = blurred[1]
    var_x = blurred[2] - mean_x * mean_x
    var_y = blurred[3] - mean_y * mean_y
    covar = blurred[4] - mean_x * mean_y
    ssim_map = (2.0 * mean_x * mean_y + 0.0001) * (2.0 * covar + 0.0009) / ((mean_x * mean_x + mean_y * mean_y + 0.0001) * (var_x + var_y + 0.0009))
    inner_x = images[..., 5:5 + row_count, :]
    inner_y = targets[..., 5:5 + row_count, :]
    return 0.8 * lax.optimization_barrier(jnp.mean(jnp.abs(inner_x - inner_y), axis=-3)) + 0.2 * (1.0 - lax.optimization_barrier(jnp.mean(ssim_map, axis=-3)))

def reference(gauss_params, visible, cameras, tile_ids, tile_blocks, target):
    half = N_CELL // 2
    quarter = N_CELL // 4
    blocks_all = gauss_params.shape[1] // GBLK
    param_blocks = gauss_params.reshape(FEAT, blocks_all, GBLK)
    seen_blocks = visible.reshape(VIEWS, blocks_all, GBLK).astype(jnp.float32)
    pixels = jnp.arange(256, dtype=jnp.int32)
    columns = jnp.arange(TILE_DEV, dtype=jnp.int32)
    across_x = (16 * columns[:, None] + pixels[None, :] % 16).astype(jnp.float32)
    images = []
    for group_id in range(N_VIEW):
        tile_list = tile_ids[:, group_id].reshape(-1)
        entry_list = tile_blocks[:, group_id].reshape(-1, LIST)
        by_tile = jnp.zeros((N_CELL * TILE_DEV, LIST), jnp.int32).at[tile_list].set(entry_list).reshape(N_CELL, TILE_DEV, LIST)

        def render_stripe(inputs):
            stripe, entries = inputs
            shifted = (stripe - quarter) % N_CELL
            view_id = 2 * group_id + shifted // half
            row_base = 16 * (shifted % half)
            across_y = jnp.broadcast_to((row_base + pixels // 16).astype(jnp.float32)[None, :], (TILE_DEV, 256))
            camera = jnp.broadcast_to(cameras[view_id][None, :], (TILE_DEV, 15))
            log_trans = jnp.zeros((TILE_DEV, 256), jnp.float32)
            colour = jnp.zeros((TILE_DEV, 3, 256), jnp.float32)
            for number in range(LIST):
                block_ids = entries[:, number]
                is_live = (block_ids >= 0).astype(jnp.float32)
                clipped = jnp.maximum(block_ids, 0)
                raw_params = jnp.moveaxis(param_blocks[:, clipped], 0, 1)
                seen_mask = seen_blocks[view_id, clipped] * is_live[:, None]
                features = project(raw_params, camera, seen_mask)
                log_trans, colour = composite(features, across_x, across_y, log_trans, colour)
            return colour
        colours = lax.map(render_stripe, (jnp.arange(N_CELL, dtype=jnp.int32), by_tile))
        images.append(colours.reshape(N_CELL, TILE_DEV, 3, 16, 16).transpose(2, 0, 3, 1, 4).reshape(3, ROWS, IMG_W))
    image = jnp.stack(images)
    moved = IMG_H // 2
    rolled_image = jnp.roll(image, -moved, axis=2)
    rolled_target = jnp.roll(target, -moved, axis=2)
    split_image = rolled_image.reshape(N_VIEW, 3, 2, IMG_H, IMG_W).transpose(0, 2, 1, 3, 4)
    split_target = rolled_target.reshape(N_VIEW, 3, 2, IMG_H, IMG_W).transpose(0, 2, 1, 3, 4)
    widths = [(0, 0), (0, 0), (0, 0), (5, 5), (0, 0)]
    loss_parts = stripe_loss(jnp.pad(split_image, widths), jnp.pad(split_target, widths), IMG_H)
    loss_map = jnp.roll(loss_parts.reshape(N_VIEW, ROWS, IMG_W), moved, axis=1)
    return (image, loss_map)
```

```python
import functools
import math

import jax
import jax.numpy as jnp
from jax import lax
from jax.experimental import pallas as pl
from jax.experimental.pallas import tpu as pltpu
from jax.sharding import PartitionSpec as P

GBLK = 128
LANES = 128
LOG2E = math.log2(math.e)
VMEM = pltpu.VMEM
SMEM = pltpu.SMEM
F32 = jnp.float32


def iota(shape, dim):
    return lax.broadcasted_iota(jnp.int32, shape, dim)


def split(value, size):
    whole = jnp.floor((value + 0.5) * (1.0 / size))
    return whole, value - whole * size


def own_route(cells, groups, blocks, cap, rcap, per_row, ids_ref, lists_ref, route_ref, box):
    length, tiles = lists_ref.shape
    box[...] = jnp.full(box.shape, -1.0, F32)
    box[0:length, 0:tiles] = lists_ref[...].astype(F32)
    box[length : length + 1, 0:tiles] = ids_ref[...].astype(F32)
    rows = box[...]
    columns = rows.T
    earlier = iota((LANES, LANES), 1) < iota((LANES, LANES), 0)

    def count(mask):
        return jnp.sum(jnp.where(mask, 1.0, 0.0), axis=1, keepdims=True)

    stripe, _ = split(columns[:, length : length + 1], per_row)
    stripe_row, _ = split(rows[length : length + 1, :], per_row)
    tile_rank = count((stripe == stripe_row) & earlier)
    owner_rows = [split(rows[n : n + 1, :], blocks)[0] for n in range(length)]
    values = []
    for n in range(length):
        entry = columns[:, n : n + 1]
        owner, _ = split(entry, blocks)
        rank = count((owner == owner_rows[n]) & earlier)
        for m in range(n):
            rank = rank + count(owner == owner_rows[m])
        values.append(jnp.where(entry >= 0.0, owner * cap + rank, -1.0))
    values.append(stripe * rcap + tile_rank)
    lane = iota((LANES, LANES), 1)
    route = jnp.zeros((LANES, LANES), F32)
    for number, value in enumerate(values):
        route = jnp.where(lane == number, value, route)
    route_ref[...] = route.T[0:8, :].astype(jnp.int32)


def harmonics(x, y, z):
    xx, yy, zz = x * x, y * y, z * z
    return [
        None,
        -0.4886025119029199 * y,
        0.4886025119029199 * z,
        -0.4886025119029199 * x,
        1.0925484305920792 * x * y,
        -1.0925484305920792 * y * z,
        0.31539156525252005 * (2.0 * zz - xx - yy),
        -1.0925484305920792 * x * z,
        0.5462742152960396 * (xx - yy),
        -0.5900435899266435 * y * (3.0 * xx - yy),
        2.890611442640554 * x * y * z,
        -0.4570457994644658 * y * (4.0 * zz - xx - yy),
        0.3731763325901154 * z * (2.0 * zz - 3.0 * xx - 3.0 * yy),
        -0.4570457994644658 * x * (4.0 * zz - xx - yy),
        1.445305721320277 * z * (xx - yy),
        -0.5900435899266435 * x * (xx - 3.0 * yy),
    ]


def view_free(param):
    mean = [param(n) for n in range(3)]
    re, qx, qy, qz = [param(6 + n) for n in range(4)]
    inv_sq = 2.0 / (re * re + qx * qx + qy * qy + qz * qz)
    sqx, sqy, sqz = qx * inv_sq, qy * inv_sq, qz * inv_sq
    xx, yy, zz = qx * sqx, qy * sqy, qz * sqz
    xy, xz, yz = qx * sqy, qx * sqz, qy * sqz
    rx, ry, rz = re * sqx, re * sqy, re * sqz
    turn = [
        [1.0 - (yy + zz), xy - rz, xz + ry],
        [xy + rz, 1.0 - (xx + zz), yz - rx],
        [xz - ry, yz + rx, 1.0 - (xx + yy)],
    ]
    scale = [jnp.exp(2.0 * param(3 + n)) for n in range(3)]
    log_opacity = -LOG2E * jnp.log(1.0 + jnp.exp(-param(10)))
    return mean, turn, scale, log_opacity


def project(param, free, cam, seen):
    mean, turn, scale, log_opacity = free
    rot = [[cam(3 * i + j) for j in range(3)] for i in range(3)]
    shift = [cam(9 + i) for i in range(3)]
    focal = cam(12)
    pc = [rot[i][0] * mean[0] + rot[i][1] * mean[1] + rot[i][2] * mean[2] + shift[i] for i in range(3)]
    inv_depth = 1.0 / pc[2]
    scaled = focal * inv_depth
    off_x = scaled * pc[0]
    off_y = scaled * pc[1]
    jac_x = off_x * inv_depth
    jac_y = off_y * inv_depth
    with_cam = [
        [scaled * rot[0][j] - jac_x * rot[2][j] for j in range(3)],
        [scaled * rot[1][j] - jac_y * rot[2][j] for j in range(3)],
    ]
    whole = [
        [sum(with_cam[i][m] * turn[m][j] for m in range(3)) for j in range(3)] for i in range(2)
    ]
    heavy = [[scale[j] * whole[i][j] for j in range(3)] for i in range(2)]
    cov_a = heavy[0][0] * whole[0][0] + heavy[0][1] * whole[0][1] + heavy[0][2] * whole[0][2] + 0.3
    cov_b = heavy[0][0] * whole[1][0] + heavy[0][1] * whole[1][1] + heavy[0][2] * whole[1][2]
    cov_c = heavy[1][0] * whole[1][0] + heavy[1][1] * whole[1][1] + heavy[1][2] * whole[1][2] + 0.3
    inv_det = LOG2E / (cov_a * cov_c - cov_b * cov_b)
    eye = [rot[0][j] * shift[0] + rot[1][j] * shift[1] + rot[2][j] * shift[2] for j in range(3)]
    head = [mean[j] + eye[j] for j in range(3)]
    inv_dist = lax.rsqrt(head[0] * head[0] + head[1] * head[1] + head[2] * head[2])
    basis = harmonics(*[part * inv_dist for part in head])
    colours = []
    for channel in range(3):
        total = 0.5 + 0.28209479177387814 * param(11 + channel)
        for j in range(1, 16):
            total = total + basis[j] * param(11 + 3 * j + channel)
        colours.append(jnp.maximum(total, 0.0))
    return [
        off_x + cam(13),
        off_y + cam(14),
        -0.5 * cov_c * inv_det,
        cov_b * inv_det,
        -0.5 * cov_a * inv_det,
        jnp.where(seen > 0, log_opacity, -1e30),
    ] + colours


def prepare_kernel(
    cells, groups, cap, rcap, per_row,
    cams_ref, ids_ref, lists_ref, params_ref, seen_ref, feats_ref, route_ref, box, stage, seen_stage,
):
    features, total = params_ref.shape
    blocks = total // GBLK
    views = seen_ref.shape[0]
    own_route(cells, groups, blocks, cap, rcap, per_row, ids_ref, lists_ref, route_ref, box)

    @pl.loop(0, -(-blocks // 8))
    def _(group):
        first = jnp.minimum(8 * group, blocks - 8)
        for b in range(8):
            lanes = pl.ds(pl.multiple_of((first + b) * GBLK, GBLK), GBLK)
            for i in range(-(-features // 8)):
                high = min(8, features - 8 * i)
                stage[pl.ds((8 * i + b) * 8, high), :] = params_ref[pl.ds(8 * i, high), lanes]
            seen_stage[pl.ds(8 * b, views), :] = seen_ref[:, lanes]

        def param(r):
            return stage[pl.ds((r // 8) * 64 + r % 8, 8, stride=8), :]

        free = view_free(param)
        for view in range(views):
            seen = seen_stage[pl.ds(view, 8, stride=8), :]
            made = project(param, free, lambda number: cams_ref[view, number], seen)
            for number, value in enumerate(made):
                feats_ref[view, number, pl.ds(first, 8), :] = value


def render_kernel(
    cells, groups, cap, rcap, per_row, blocks,
    me_ref, table_ref, feats_ref, early_up, early_down, out_ref, code_ref,
    box, info, turned, shades, rest, sheets, code_box, code_smem, sem,
):
    del early_up, early_down
    devices = cells * groups
    quarter, half = cells // 4, cells // 2
    length, tiles = table_ref.shape[1] - 1, table_ref.shape[2]
    views = feats_ref.shape[0]
    box[...] = jnp.full(box.shape, -1.0, F32)
    for n in range(length + 1):
        box[n, :, 0:tiles] = table_ref[:, n, :].astype(F32)
    me = me_ref[0].astype(F32)
    my_stripe = me_ref[1].astype(F32)
    before = jnp.where(iota((LANES, LANES), 0) < iota((LANES, LANES), 1), 1.0, 0.0)

    def ranks(mask):
        ones = jnp.where(mask, 1.0, 0.0)
        return jnp.dot(ones, before, preferred_element_type=F32), jnp.sum(ones, axis=1, keepdims=True)

    def pick(mask, value):
        return jnp.sum(jnp.where(mask, value, 0.0), axis=1, keepdims=True)

    stripe, column = split(box[length], per_row)
    shifted = stripe - quarter
    shifted = jnp.where(shifted < 0.0, shifted + cells, shifted)
    group_of = jnp.bitwise_and(iota((devices, 1), 0), groups - 1).astype(F32)
    tile_code = column + 128.0 * shifted + 16384.0 * group_of
    code_lane = iota((devices, LANES), 1)
    codes = jnp.zeros((devices, LANES), F32)
    prior = jnp.zeros((devices, 1), F32)
    mine = []
    for n in range(length):
        owner, local_slot = split(box[n], blocks)
        hit = owner == me
        rank, total = ranks(hit)
        mine.append((hit, rank + prior, local_slot))
        prior = prior + total
    slot_lane = iota((devices, 2 * LANES), 1).astype(F32)
    found = jnp.zeros((1, 2 * LANES), F32)
    for k in range(cap):
        asked = sum(pick(hit & (rank == k), local_slot + 1.0) for hit, rank, local_slot in mine)
        tile = sum(pick(hit & (rank == k), tile_code) for hit, rank, local_slot in mine)
        codes = jnp.where(code_lane == k, asked, codes)
        found = found + jnp.sum(jnp.where(slot_lane == asked - 1.0, tile, 0.0), axis=0, keepdims=True)
    here = stripe == my_stripe
    rank, _ = ranks(here)
    for k in range(rcap):
        codes = jnp.where(code_lane == cap + k, pick(here & (rank == k), column + 1.0), codes)
    code_box[...] = codes.astype(jnp.int32)
    code_ref[...] = codes.astype(jnp.int32)
    scalars = pltpu.make_async_copy(code_box, code_smem, sem)
    scalars.start()

    for part in range(2):
        row = found[:, part * LANES : (part + 1) * LANES]
        info[pl.ds(part * LANES, LANES), :] = jnp.broadcast_to(row, (LANES, LANES)).T
    for part in range(2):
        count = (LANES, 32)[part]
        rows = pl.ds(part * LANES, count)
        tile = info[rows, :].astype(jnp.int32)
        column = jnp.bitwise_and(tile, 127)
        shifted = jnp.bitwise_and(tile >> 7, 127)
        side = (shifted >= half).astype(jnp.int32)
        view = 2 * (tile >> 14) + side
        anchors = [(16 * column).astype(F32), (16 * (shifted - side * half)).astype(F32)]
        is_view = [view == w for w in range(1, views)]
        for number in range(9):
            value = feats_ref[0, number, rows, :]
            for w in range(1, views):
                value = jnp.where(is_view[w - 1], feats_ref[w, number, rows, :], value)
            if number < 2:
                value = value - anchors[number]
            if part == 1:
                value = jnp.concatenate([value] * 4, axis=0)
            turned[part, number] = value.T

    across = [iota((8, LANES), 0).astype(F32) + 8.0 * xh for xh in range(2)]
    unroll = 4

    def composite(part, pixel_rows):
        def steps(n, carry):
            trans = list(carry[0])
            colour = [list(rows) for rows in carry[1]]
            for u in range(unroll):
                sx, sy, ca, cb, cc, lo, *shade = [
                    jnp.broadcast_to(turned[part, f, pl.ds(unroll * n + u, 1), :], (8, LANES))
                    for f in range(9)
                ]
                dx = [across[xh] - sx for xh in range(2)]
                flat = [ca * dx[xh] * dx[xh] + lo for xh in range(2)]
                mixed = [cb * dx[xh] for xh in range(2)]
                for yl in range(4):
                    dy = pixel_rows[yl] - sy
                    bend = cc * dy
                    for xh in range(2):
                        v = 2 * yl + xh
                        weight = jnp.exp2(flat[xh] + dy * (mixed[xh] + bend)) * trans[v]
                        trans[v] = trans[v] - weight
                        for c in range(3):
                            colour[c][v] = colour[c][v] + weight * shade[c]
            return tuple(trans), tuple(tuple(rows) for rows in colour)

        zero = jnp.zeros((8, LANES), F32)
        start = (tuple(zero + 1.0 for _ in range(8)), tuple(tuple(zero for _ in range(8)) for _ in range(3)))
        trans, colour = lax.fori_loop(0, GBLK // unroll, steps, start)
        return [*colour, trans]

    @pl.loop(0, 4)
    def _(chunk):
        high, odd = chunk >> 1, jnp.bitwise_and(chunk, 1)
        pixel_rows = [
            (8 * high + jnp.bitwise_and(8 - 4 * odd - yl, 7)).astype(F32) for yl in range(4)
        ]
        planes = composite(0, pixel_rows)
        for c in range(4):
            for v in range(8):
                shades[pl.ds(c * 256 + chunk * 64 + 8 * v, 8), :] = planes[c][v]

    chunk = iota((8, LANES), 1) >> 5
    high, odd = chunk >> 1, jnp.bitwise_and(chunk, 1)
    pixel_rows = [
        (8 * high + jnp.bitwise_and(8 - 4 * odd - yl, 7)).astype(F32) for yl in range(4)
    ]
    planes = composite(1, pixel_rows)
    for c in range(4):
        for v in range(8):
            rest[pl.ds(c * 64 + 8 * v, 8), :] = planes[c][v]

    for r in range(8):
        sheets[pl.ds(r, LANES, stride=8), :] = shades[pl.ds(r * LANES, LANES), :].T
    left = iota((32, LANES), 1) < 64
    for pair in range(2):
        both = rest[pl.ds(pair * LANES, LANES), :].T
        parts = [both[32 * q : 32 * q + 32, :] for q in range(4)]
        swapped = [pltpu.roll(part, 64, 1) for part in parts]
        for h in range(2):
            low = jnp.where(left, parts[2 * h], swapped[2 * h + 1])
            high = jnp.where(left, swapped[2 * h], parts[2 * h + 1])
            sheets[pl.ds(LANES * 8 + 4 * pair + h, 32, stride=8), :] = low
            sheets[pl.ds(LANES * 8 + 4 * pair + 2 + h, 32, stride=8), :] = high
    scalars.wait()

    @pl.loop(0, devices)
    def _(d):
        for k in range(cap):
            place = jnp.clip(code_smem[d, k] - 1, 0, blocks - 1)
            out_ref[d, pl.ds(8 * k, 8), :] = sheets[pl.ds(pl.multiple_of(8 * place, 8), 8), :]


def combine_kernel(tiles, route_ref, got_ref, fixed_ref, out_ref):
    del fixed_ref
    line = iota((8, LANES), 0)

    @pl.loop(0, tiles, unroll=8)
    def _(t):
        front = route_ref[0, t]
        back = route_ref[1, t]
        where_to = route_ref[2, t]
        near = got_ref[pl.ds(pl.multiple_of(8 * front, 8), 8), :]
        far = got_ref[pl.ds(pl.multiple_of(8 * jnp.maximum(back, 0), 8), 8), :]
        keep = jnp.where(line >= 6, near, 0.0)
        keep = keep + pltpu.roll(keep, 4, 0)
        keep = keep + pltpu.roll(keep, 2, 0)
        tile = near + jnp.where(back >= 0, keep * far, 0.0)
        out_ref[pl.ds(6 * where_to, 6), :] = tile[0:6, :]


def place_kernel(
    groups, cap, rcap, per_row, code_ref, me_ref, got_ref, image_ref, head_ref, tail_ref, board
):
    cells = got_ref.shape[0]

    @pl.loop(0, cells)
    def _(cell):
        for k in range(rcap):
            column = code_ref[cell * groups + me_ref[2], cap + k] - 1
            spot = jnp.where(column < 0, per_row, column)
            board[pl.ds(8 * spot, 6), :] = got_ref[cell, 6 * k : 6 * k + 6, :]

    group = iota((8, LANES), 1) >> 4
    masks = [jnp.bitwise_and(group, bit) != 0 for bit in (1, 2, 4)]
    for j in range(per_row // 8):
        for c in range(3):
            for h in range(2):
                made = board[pl.ds(64 * j + 2 * c + h, 8, stride=8), :]
                made = pltpu.roll(made, 0, 1, stride=16, stride_axis=0)
                for mask, bit in zip(masks, (1, 2, 4)):
                    made = jnp.where(mask, pltpu.roll(made, 8 - bit, 0), made)
                made = pltpu.roll(made, 0, 1, stride=16, stride_axis=0)
                image_ref[0, c, 8 * h : 8 * h + 8, 128 * j : 128 * j + 128] = made
    head_ref[...] = image_ref[0, :, 0:5, :]
    tail_ref[...] = image_ref[0, :, 11:16, :]


def window_taps():
    raw = [math.exp(-k * k / 4.5) for k in range(6)]
    whole = raw[0] + 2.0 * sum(raw[1:])
    return [value / whole for value in raw]


def across_rows(tall, first, count):
    taps = window_taps()
    around = (count + 2) * LANES
    blurred = []
    for f in range(tall.shape[0]):
        given = tall[f, :, LANES * first : LANES * first + around]
        total = taps[0] * given
        for k in range(1, 6):
            total = total + taps[k] * (pltpu.roll(given, k, 1) + pltpu.roll(given, around - k, 1))
        blurred.append(total[:, LANES : LANES + count * LANES])
    return blurred


def clear_sides(tall):
    blank = jnp.zeros((tall.shape[0], 16, LANES), F32)
    tall[:, :, 0:LANES] = blank
    tall[:, :, tall.shape[2] - LANES :] = blank


def down_columns(fields, f):
    taps = window_taps()
    total = taps[0] * fields[f, 5:21, :]
    for k in range(1, 6):
        total = total + taps[k] * (fields[f, 5 - k : 21 - k, :] + fields[f, 5 + k : 21 + k, :])
    return total


def span(j):
    return pl.ds(pl.multiple_of(LANES * j, LANES), LANES)


RUN = 5


def target_kernel(target_ref, up_ref, down_ref, late_ref, out_ref, fields, tall):
    del late_ref
    spans = target_ref.shape[3] // LANES
    clear_sides(tall)

    @pl.loop(0, 3)
    def _(c):
        @pl.loop(0, spans)
        def _(j):
            fields[0, 0:5, :] = up_ref[c, :, span(j)]
            fields[0, 5:21, :] = target_ref[0, c, :, span(j)]
            fields[0, 21:26, :] = down_ref[c, :, span(j)]
            fields[1] = fields[0] * fields[0]
            for f in range(2):
                tall[f, :, span(j + 1)] = down_columns(fields, f)

        for first in range(0, spans, RUN):
            count = min(RUN, spans - first)
            for f, value in enumerate(across_rows(tall, first, count)):
                out_ref[f, c, :, LANES * first : LANES * (first + count)] = value


def own_kernel(image_ref, target_ref, out_ref, fields, tall):
    spans = target_ref.shape[3] // LANES
    clear_sides(tall)
    fields[...] = jnp.zeros(fields.shape, F32)

    @pl.loop(0, 3)
    def _(c):
        @pl.loop(0, spans)
        def _(j):
            x = image_ref[0, c, :, span(j)]
            y = target_ref[0, c, :, span(j)]
            fields[0, 5:21, :] = x
            fields[1, 5:21, :] = x * x
            fields[2, 5:21, :] = x * y
            for f in range(3):
                tall[f, :, span(j + 1)] = down_columns(fields, f)

        for first in range(0, spans, RUN):
            count = min(RUN, spans - first)
            for f, value in enumerate(across_rows(tall, first, count)):
                out_ref[f, c, :, LANES * first : LANES * (first + count)] = value


def loss_kernel(
    image_ref, target_ref, own_ref, fixed_ref, up_ref, down_ref, target_up, target_down,
    image_out, loss_ref, fields, tall,
):
    taps = window_taps()
    image_out[...] = image_ref[...]
    spans = image_ref.shape[3] // LANES
    clear_sides(tall)
    fields[...] = jnp.zeros(fields.shape, F32)

    @pl.loop(0, 3)
    def _(c):
        @pl.loop(0, spans)
        def _(j):
            x = up_ref[c, :, span(j)]
            y = target_up[c, :, span(j)]
            for f, value in enumerate((x, x * x, x * y)):
                fields[f, 3:8, :] = value
            x = down_ref[c, :, span(j)]
            y = target_down[c, :, span(j)]
            for f, value in enumerate((x, x * x, x * y)):
                fields[f, 24:29, :] = value
            for f in range(3):
                above = taps[1] * fields[f, 7:15, :]
                below = taps[1] * fields[f, 17:25, :]
                for k in range(2, 6):
                    above = above + taps[k] * fields[f, 8 - k : 16 - k, :]
                    below = below + taps[k] * fields[f, 16 + k : 24 + k, :]
                tall[f, 0:8, span(j + 1)] = above
                tall[f, 8:16, span(j + 1)] = below

        for first in range(0, spans, RUN):
            count = min(RUN, spans - first)
            lanes = slice(LANES * first, LANES * (first + count))
            mx, xx, xy = [
                value + own_ref[f, c, :, lanes]
                for f, value in enumerate(across_rows(tall, first, count))
            ]
            my = fixed_ref[0, c, :, lanes]
            both = mx * my
            sums = mx * mx + my * my
            ssim = (2.0 * both + 0.0001) * (2.0 * (xy - both) + 0.0009) / (
                (sums + 0.0001) * (xx + fixed_ref[1, c, :, lanes] - sums + 0.0009)
            )
            gap = jnp.abs(image_ref[0, c, :, lanes] - target_ref[0, c, :, lanes])
            part = (0.8 / 3.0) * gap - (0.2 / 3.0) * ssim
            loss_ref[0, :, lanes] = jnp.where(c == 0, 0.2, loss_ref[0, :, lanes]) + part


def call(kernel, outs, specs, scratch=(), mem=16, work=0):
    return pl.pallas_call(
        kernel,
        out_shape=outs,
        in_specs=[pl.BlockSpec(memory_space=spec) for spec in specs],
        scratch_shapes=list(scratch),
        cost_estimate=pl.CostEstimate(flops=work, bytes_accessed=0, transcendentals=0) if work else None,
        compiler_params=pltpu.CompilerParams(vmem_limit_bytes=mem * 2**20),
    )


def local(gauss_params, visible, cameras, tile_ids, tile_blocks, target):
    cells = lax.axis_size("cell")
    groups = lax.axis_size("view")
    devices = cells * groups
    half = cells // 2
    quarter = cells // 4
    blocks = gauss_params.shape[1] // GBLK
    cap = -(-blocks // devices)
    width = target.shape[3]
    per_row = width // 16
    tiles = tile_ids.shape[2]
    rcap = -(-tiles // cells)
    length = tile_blocks.shape[3]
    rows = LANES + 32
    shape = jax.ShapeDtypeStruct
    my_cell = lax.axis_index("cell").astype(jnp.int32)
    my_view = lax.axis_index("view").astype(jnp.int32)
    me = jnp.stack([my_cell * groups + my_view, my_cell, my_view])
    down_pairs = [(s, (s + 1) % cells) for s in range(cells) if (s - quarter) % half != half - 1]
    up_pairs = [(b, a) for a, b in down_pairs]
    target_up = lax.ppermute(target[0, :, 11:16, :], "cell", down_pairs)
    target_down = lax.ppermute(target[0, :, 0:5, :], "cell", up_pairs)

    lists = jnp.swapaxes(tile_blocks[0, 0], 0, 1)
    table = jnp.concatenate([lists, tile_ids[0]], axis=0)
    table = lax.all_to_all(
        jnp.broadcast_to(table, (devices, length + 1, tiles)),
        ("cell", "view"), split_axis=0, concat_axis=0, tiled=True,
    )
    work = blocks * GBLK * 10000
    feats, route = call(
        functools.partial(prepare_kernel, cells, groups, cap, rcap, per_row),
        (shape((visible.shape[0], 9, rows, GBLK), F32), shape((8, LANES), jnp.int32)),
        [SMEM] + [VMEM] * 4,
        [VMEM((LANES, LANES), F32), VMEM((512, LANES), F32), VMEM((64, LANES), jnp.int32)],
        32, work,
    )(cameras, tile_ids[0], lists, gauss_params, visible)
    made, code = call(
        functools.partial(render_kernel, cells, groups, cap, rcap, per_row, blocks),
        (shape((devices, 8 * cap, LANES), F32), shape((devices, LANES), jnp.int32)),
        [SMEM, VMEM, VMEM, pl.ANY, pl.ANY],
        [
            VMEM((length + 1, devices, LANES), F32),
            VMEM((2 * LANES, LANES), F32),
            VMEM((2, 9, LANES, LANES), F32),
            VMEM((1024, LANES), F32),
            VMEM((256, LANES), F32),
            VMEM((rows * 8, LANES), F32),
            VMEM((devices, LANES), jnp.int32),
            SMEM((devices, LANES), jnp.int32),
            pltpu.SemaphoreType.DMA,
        ],
        32, work,
    )(me, table, feats, target_up, target_down)
    got = lax.all_to_all(made, ("cell", "view"), split_axis=0, concat_axis=0, tiled=True)
    planes = shape((1, 3, 16, width), F32)
    fixed = call(
        target_kernel,
        shape((2, 3, 16, width), F32),
        [VMEM] * 3 + [pl.ANY],
        [VMEM((2, 32, LANES), F32), VMEM((2, 16, width + 2 * LANES), F32)],
        16, work,
    )(target, target_up, target_down, made)
    tile_rows = call(
        functools.partial(combine_kernel, tiles),
        shape((cells * 6 * rcap, LANES), F32),
        [SMEM, VMEM, pl.ANY],
    )(route, got.reshape(devices * cap * 8, LANES), fixed)
    got_tiles = lax.all_to_all(
        tile_rows.reshape(cells, 6 * rcap, LANES), "cell", split_axis=0, concat_axis=0, tiled=True
    )
    edge = shape((3, 5, width), F32)
    image, head, tail = call(
        functools.partial(place_kernel, groups, cap, rcap, per_row),
        (planes, edge, edge),
        [SMEM, SMEM, VMEM],
        [VMEM((8 * (per_row + 1), LANES), F32)],
    )(code, me, got_tiles)
    up_rows = lax.ppermute(tail, "cell", down_pairs)
    down_rows = lax.ppermute(head, "cell", up_pairs)
    blur_room = [VMEM((3, 32, LANES), F32), VMEM((3, 16, width + 2 * LANES), F32)]
    own = call(
        own_kernel, shape((3, 3, 16, width), F32), [VMEM] * 2, blur_room, 16, work
    )(image, target)
    return call(
        loss_kernel, (planes, shape((1, 16, width), F32)), [VMEM] * 8, blur_room, 24
    )(image, target, own, fixed, up_rows, down_rows, target_up, target_down)


def solution(mesh):
    return jax.shard_map(
        local,
        mesh=mesh,
        in_specs=(
            P(None, ("cell", "view")),
            P(None, ("cell", "view")),
            P(),
            P("cell", "view", None),
            P("cell", "view", None, None),
            P("view", None, "cell", None),
        ),
        out_specs=(P("view", None, "cell", None), P("view", "cell", None)),
        check_vma=False,
    )
```

```python
import functools
import math

import jax
import jax.numpy as jnp
from jax import lax
from jax.experimental import pallas as pl
from jax.experimental.pallas import tpu as pltpu
from jax.sharding import PartitionSpec as P

GBLK = 128
LANES = 128
LOG2E = math.log2(math.e)
VMEM = pltpu.VMEM
SMEM = pltpu.SMEM
HBM = pltpu.HBM
PIECES = 4
F32 = jnp.float32


def iota(shape, dim):
    return lax.broadcasted_iota(jnp.int32, shape, dim)


def split(value, size):
    whole = jnp.floor((value + 0.5) * (1.0 / size))
    return whole, value - whole * size


def own_route(cells, groups, blocks, cap, rcap, per_row, table_ref, route_ref, box):
    length, tiles = table_ref.shape[0] - 1, table_ref.shape[1]
    box[...] = jnp.full(box.shape, -1.0, F32)
    box[0 : length + 1, 0:tiles] = table_ref[...].astype(F32)
    rows = box[...]
    columns = rows.T
    earlier = iota((LANES, LANES), 1) < iota((LANES, LANES), 0)

    def count(mask):
        return jnp.sum(jnp.where(mask, 1.0, 0.0), axis=1, keepdims=True)

    stripe, _ = split(columns[:, length : length + 1], per_row)
    stripe_row, _ = split(rows[length : length + 1, :], per_row)
    tile_rank = count((stripe == stripe_row) & earlier)
    owner_rows = [split(rows[n : n + 1, :], blocks)[0] for n in range(length)]
    values = []
    for n in range(length):
        entry = columns[:, n : n + 1]
        owner, _ = split(entry, blocks)
        rank = count((owner == owner_rows[n]) & earlier)
        for m in range(n):
            rank = rank + count(owner == owner_rows[m])
        values.append(jnp.where(entry >= 0.0, owner * cap + rank, -1.0))
    values.append(stripe * rcap + tile_rank)
    lane = iota((LANES, LANES), 1)
    route = jnp.zeros((LANES, LANES), F32)
    for number, value in enumerate(values):
        route = jnp.where(lane == number, value, route)
    route_ref[...] = route.T[0:8, :].astype(jnp.int32)


def harmonics(x, y, z):
    xx, yy, zz = x * x, y * y, z * z
    return [
        None,
        -0.4886025119029199 * y,
        0.4886025119029199 * z,
        -0.4886025119029199 * x,
        1.0925484305920792 * x * y,
        -1.0925484305920792 * y * z,
        0.31539156525252005 * (2.0 * zz - xx - yy),
        -1.0925484305920792 * x * z,
        0.5462742152960396 * (xx - yy),
        -0.5900435899266435 * y * (3.0 * xx - yy),
        2.890611442640554 * x * y * z,
        -0.4570457994644658 * y * (4.0 * zz - xx - yy),
        0.3731763325901154 * z * (2.0 * zz - 3.0 * xx - 3.0 * yy),
        -0.4570457994644658 * x * (4.0 * zz - xx - yy),
        1.445305721320277 * z * (xx - yy),
        -0.5900435899266435 * x * (xx - 3.0 * yy),
    ]


def view_free(param):
    mean = [param(n) for n in range(3)]
    re, qx, qy, qz = [param(6 + n) for n in range(4)]
    inv_sq = 2.0 / (re * re + qx * qx + qy * qy + qz * qz)
    sqx, sqy, sqz = qx * inv_sq, qy * inv_sq, qz * inv_sq
    xx, yy, zz = qx * sqx, qy * sqy, qz * sqz
    xy, xz, yz = qx * sqy, qx * sqz, qy * sqz
    rx, ry, rz = re * sqx, re * sqy, re * sqz
    turn = [
        [1.0 - (yy + zz), xy - rz, xz + ry],
        [xy + rz, 1.0 - (xx + zz), yz - rx],
        [xz - ry, yz + rx, 1.0 - (xx + yy)],
    ]
    scale = [jnp.exp(2.0 * param(3 + n)) for n in range(3)]
    log_opacity = -LOG2E * jnp.log(1.0 + jnp.exp(-param(10)))
    return mean, turn, scale, log_opacity


def project(param, free, cam, seen):
    mean, turn, scale, log_opacity = free
    rot = [[cam(3 * i + j) for j in range(3)] for i in range(3)]
    shift = [cam(9 + i) for i in range(3)]
    focal = cam(12)
    pc = [rot[i][0] * mean[0] + rot[i][1] * mean[1] + rot[i][2] * mean[2] + shift[i] for i in range(3)]
    inv_depth = 1.0 / pc[2]
    scaled = focal * inv_depth
    off_x = scaled * pc[0]
    off_y = scaled * pc[1]
    jac_x = off_x * inv_depth
    jac_y = off_y * inv_depth
    with_cam = [
        [scaled * rot[0][j] - jac_x * rot[2][j] for j in range(3)],
        [scaled * rot[1][j] - jac_y * rot[2][j] for j in range(3)],
    ]
    whole = [
        [sum(with_cam[i][m] * turn[m][j] for m in range(3)) for j in range(3)] for i in range(2)
    ]
    heavy = [[scale[j] * whole[i][j] for j in range(3)] for i in range(2)]
    cov_a = heavy[0][0] * whole[0][0] + heavy[0][1] * whole[0][1] + heavy[0][2] * whole[0][2] + 0.3
    cov_b = heavy[0][0] * whole[1][0] + heavy[0][1] * whole[1][1] + heavy[0][2] * whole[1][2]
    cov_c = heavy[1][0] * whole[1][0] + heavy[1][1] * whole[1][1] + heavy[1][2] * whole[1][2] + 0.3
    inv_det = LOG2E / (cov_a * cov_c - cov_b * cov_b)
    eye = [rot[0][j] * shift[0] + rot[1][j] * shift[1] + rot[2][j] * shift[2] for j in range(3)]
    head = [mean[j] + eye[j] for j in range(3)]
    inv_dist = lax.rsqrt(head[0] * head[0] + head[1] * head[1] + head[2] * head[2])
    basis = harmonics(*[part * inv_dist for part in head])
    colours = []
    for channel in range(3):
        total = 0.5 + 0.28209479177387814 * param(11 + channel)
        for j in range(1, 16):
            total = total + basis[j] * param(11 + 3 * j + channel)
        colours.append(jnp.maximum(total, 0.0))
    return [
        off_x + cam(13),
        off_y + cam(14),
        -0.5 * cov_c * inv_det,
        cov_b * inv_det,
        -0.5 * cov_a * inv_det,
        jnp.where(seen > 0, log_opacity, -1e30),
    ] + colours


def prepare_kernel(
    cells, groups, cap, rcap, per_row,
    cams_ref, table_ref, params_hbm, seen_hbm, feats_ref, route_ref,
    box, stage, seen_stage, params_ref, seen_ref, sems,
):
    features, total = params_ref.shape
    blocks = total // GBLK
    views = seen_ref.shape[0]
    seen_copy = pltpu.make_async_copy(seen_hbm, seen_ref, sems.at[PIECES])
    seen_copy.start()
    groups_all = -(-blocks // 8)
    per_piece = -(-groups_all // PIECES)
    copies = []
    for piece in range(PIECES):
        low = piece * per_piece * 8 * GBLK
        lanes = pl.ds(low, min(per_piece * 8 * GBLK, total - low))
        copies.append(
            pltpu.make_async_copy(params_hbm.at[:, lanes], params_ref.at[:, lanes], sems.at[piece])
        )
        copies[-1].start()
    own_route(cells, groups, blocks, cap, rcap, per_row, table_ref, route_ref, box)
    seen_copy.wait()

    def project_group(group):
        first = jnp.minimum(8 * group, blocks - 8)
        for b in range(8):
            lanes = pl.ds(pl.multiple_of((first + b) * GBLK, GBLK), GBLK)
            for i in range(-(-features // 8)):
                high = min(8, features - 8 * i)
                stage[pl.ds((8 * i + b) * 8, high), :] = params_ref[pl.ds(8 * i, high), lanes]
            seen_stage[pl.ds(8 * b, views), :] = seen_ref[:, lanes]

        def param(r):
            return stage[pl.ds((r // 8) * 64 + r % 8, 8, stride=8), :]

        free = view_free(param)
        for view in range(views):
            seen = seen_stage[pl.ds(view, 8, stride=8), :]
            made = project(param, free, lambda number: cams_ref[view, number], seen)
            for number, value in enumerate(made):
                feats_ref[view, number, pl.ds(first, 8), :] = value

    for piece in range(PIECES):
        copies[piece].wait()
        pl.loop(piece * per_piece, min((piece + 1) * per_piece, groups_all))(project_group)


def render_kernel(
    cells, groups, cap, rcap, per_row, blocks,
    me_ref, table_ref, feats_ref, target_ref, out_ref, code_ref, head_ref, tail_ref,
    box, info, turned, shades, rest, sheets, code_box, code_smem, sem,
):
    head_ref[...] = target_ref[0, :, 0:5, :]
    tail_ref[...] = target_ref[0, :, 11:16, :]
    devices = cells * groups
    quarter, half = cells // 4, cells // 2
    length, tiles = table_ref.shape[1] - 1, table_ref.shape[2]
    views = feats_ref.shape[0]
    box[...] = jnp.full(box.shape, -1.0, F32)
    for n in range(length + 1):
        box[n, :, 0:tiles] = table_ref[:, n, :].astype(F32)
    me = me_ref[0].astype(F32)
    my_stripe = me_ref[1].astype(F32)
    before = jnp.where(iota((LANES, LANES), 0) < iota((LANES, LANES), 1), 1.0, 0.0)

    def ranks(mask):
        ones = jnp.where(mask, 1.0, 0.0)
        return jnp.dot(ones, before, preferred_element_type=F32), jnp.sum(ones, axis=1, keepdims=True)

    def pick(mask, value):
        return jnp.sum(jnp.where(mask, value, 0.0), axis=1, keepdims=True)

    stripe, column = split(box[length], per_row)
    shifted = stripe - quarter
    shifted = jnp.where(shifted < 0.0, shifted + cells, shifted)
    group_of = jnp.bitwise_and(iota((devices, 1), 0), groups - 1).astype(F32)
    tile_code = column + 128.0 * shifted + 16384.0 * group_of
    code_lane = iota((devices, LANES), 1)
    codes = jnp.zeros((devices, LANES), F32)
    prior = jnp.zeros((devices, 1), F32)
    mine = []
    for n in range(length):
        owner, local_slot = split(box[n], blocks)
        hit = owner == me
        rank, total = ranks(hit)
        mine.append((hit, rank + prior, local_slot))
        prior = prior + total
    slot_lane = iota((devices, 2 * LANES), 1).astype(F32)
    found = jnp.zeros((1, 2 * LANES), F32)
    for k in range(cap):
        asked = sum(pick(hit & (rank == k), local_slot + 1.0) for hit, rank, local_slot in mine)
        tile = sum(pick(hit & (rank == k), tile_code) for hit, rank, local_slot in mine)
        codes = jnp.where(code_lane == k, asked, codes)
        found = found + jnp.sum(jnp.where(slot_lane == asked - 1.0, tile, 0.0), axis=0, keepdims=True)
    here = stripe == my_stripe
    rank, _ = ranks(here)
    for k in range(rcap):
        codes = jnp.where(code_lane == cap + k, pick(here & (rank == k), column + 1.0), codes)
    code_box[...] = codes.astype(jnp.int32)
    code_ref[...] = codes.astype(jnp.int32)
    scalars = pltpu.make_async_copy(code_box, code_smem, sem)
    scalars.start()

    for part in range(2):
        row = found[:, part * LANES : (part + 1) * LANES]
        info[pl.ds(part * LANES, LANES), :] = jnp.broadcast_to(row, (LANES, LANES)).T
    for part in range(2):
        count = (LANES, 32)[part]
        rows = pl.ds(part * LANES, count)
        tile = info[rows, :].astype(jnp.int32)
        column = jnp.bitwise_and(tile, 127)
        shifted = jnp.bitwise_and(tile >> 7, 127)
        side = (shifted >= half).astype(jnp.int32)
        view = 2 * (tile >> 14) + side
        anchors = [(16 * column).astype(F32), (16 * (shifted - side * half)).astype(F32)]
        is_view = [view == w for w in range(1, views)]
        for number in range(9):
            value = feats_ref[0, number, rows, :]
            for w in range(1, views):
                value = jnp.where(is_view[w - 1], feats_ref[w, number, rows, :], value)
            if number < 2:
                value = value - anchors[number]
            if part == 1:
                value = jnp.concatenate([value] * 4, axis=0)
            turned[part, number] = value.T

    across = [iota((8, LANES), 0).astype(F32) + 8.0 * xh for xh in range(2)]
    unroll = 4

    def composite(part, pixel_rows):
        def steps(n, carry):
            trans = list(carry[0])
            colour = [list(rows) for rows in carry[1]]
            for u in range(unroll):
                sx, sy, ca, cb, cc, lo, *shade = [
                    jnp.broadcast_to(turned[part, f, pl.ds(unroll * n + u, 1), :], (8, LANES))
                    for f in range(9)
                ]
                dx = [across[xh] - sx for xh in range(2)]
                flat = [ca * dx[xh] * dx[xh] + lo for xh in range(2)]
                mixed = [cb * dx[xh] for xh in range(2)]
                for yl in range(4):
                    dy = pixel_rows[yl] - sy
                    bend = cc * dy
                    for xh in range(2):
                        v = 2 * yl + xh
                        weight = jnp.exp2(flat[xh] + dy * (mixed[xh] + bend)) * trans[v]
                        trans[v] = trans[v] - weight
                        for c in range(3):
                            colour[c][v] = colour[c][v] + weight * shade[c]
            return tuple(trans), tuple(tuple(rows) for rows in colour)

        zero = jnp.zeros((8, LANES), F32)
        start = (tuple(zero + 1.0 for _ in range(8)), tuple(tuple(zero for _ in range(8)) for _ in range(3)))
        trans, colour = lax.fori_loop(0, GBLK // unroll, steps, start)
        return [*colour, trans]

    @pl.loop(0, 4)
    def _(chunk):
        high, odd = chunk >> 1, jnp.bitwise_and(chunk, 1)
        pixel_rows = [
            (8 * high + jnp.bitwise_and(8 - 4 * odd - yl, 7)).astype(F32) for yl in range(4)
        ]
        planes = composite(0, pixel_rows)
        for c in range(4):
            for v in range(8):
                shades[pl.ds(c * 256 + chunk * 64 + 8 * v, 8), :] = planes[c][v]

    chunk = iota((8, LANES), 1) >> 5
    high, odd = chunk >> 1, jnp.bitwise_and(chunk, 1)
    pixel_rows = [
        (8 * high + jnp.bitwise_and(8 - 4 * odd - yl, 7)).astype(F32) for yl in range(4)
    ]
    planes = composite(1, pixel_rows)
    for c in range(4):
        for v in range(8):
            rest[pl.ds(c * 64 + 8 * v, 8), :] = planes[c][v]

    for r in range(8):
        sheets[pl.ds(r, LANES, stride=8), :] = shades[pl.ds(r * LANES, LANES), :].T
    left = iota((32, LANES), 1) < 64
    for pair in range(2):
        both = rest[pl.ds(pair * LANES, LANES), :].T
        parts = [both[32 * q : 32 * q + 32, :] for q in range(4)]
        swapped = [pltpu.roll(part, 64, 1) for part in parts]
        for h in range(2):
            low = jnp.where(left, parts[2 * h], swapped[2 * h + 1])
            high = jnp.where(left, swapped[2 * h], parts[2 * h + 1])
            sheets[pl.ds(LANES * 8 + 4 * pair + h, 32, stride=8), :] = low
            sheets[pl.ds(LANES * 8 + 4 * pair + 2 + h, 32, stride=8), :] = high
    scalars.wait()

    @pl.loop(0, devices)
    def _(d):
        for k in range(cap):
            place = jnp.clip(code_smem[d, k] - 1, 0, blocks - 1)
            out_ref[d, pl.ds(8 * k, 8), :] = sheets[pl.ds(pl.multiple_of(8 * place, 8), 8), :]


def combine_kernel(tiles, route_ref, got_ref, fixed_ref, out_ref):
    del fixed_ref
    line = iota((8, LANES), 0)

    @pl.loop(0, tiles, unroll=8)
    def _(t):
        front = route_ref[0, t]
        back = route_ref[1, t]
        where_to = route_ref[2, t]
        near = got_ref[pl.ds(pl.multiple_of(8 * front, 8), 8), :]
        far = got_ref[pl.ds(pl.multiple_of(8 * jnp.maximum(back, 0), 8), 8), :]
        keep = jnp.where(line >= 6, near, 0.0)
        keep = keep + pltpu.roll(keep, 4, 0)
        keep = keep + pltpu.roll(keep, 2, 0)
        tile = near + jnp.where(back >= 0, keep * far, 0.0)
        out_ref[pl.ds(6 * where_to, 6), :] = tile[0:6, :]


def place_kernel(
    groups, cap, rcap, per_row, code_ref, me_ref, got_ref, image_ref, head_ref, tail_ref, board
):
    cells = got_ref.shape[0]

    @pl.loop(0, cells)
    def _(cell):
        for k in range(rcap):
            column = code_ref[cell * groups + me_ref[2], cap + k] - 1
            spot = jnp.where(column < 0, per_row, column)
            board[pl.ds(8 * spot, 6), :] = got_ref[cell, 6 * k : 6 * k + 6, :]

    group = iota((8, LANES), 1) >> 4
    masks = [jnp.bitwise_and(group, bit) != 0 for bit in (1, 2, 4)]
    for j in range(per_row // 8):
        for c in range(3):
            for h in range(2):
                made = board[pl.ds(64 * j + 2 * c + h, 8, stride=8), :]
                made = pltpu.roll(made, 0, 1, stride=16, stride_axis=0)
                for mask, bit in zip(masks, (1, 2, 4)):
                    made = jnp.where(mask, pltpu.roll(made, 8 - bit, 0), made)
                made = pltpu.roll(made, 0, 1, stride=16, stride_axis=0)
                image_ref[0, c, 8 * h : 8 * h + 8, 128 * j : 128 * j + 128] = made
    head_ref[...] = image_ref[0, :, 0:5, :]
    tail_ref[...] = image_ref[0, :, 11:16, :]


def window_taps():
    raw = [math.exp(-k * k / 4.5) for k in range(6)]
    whole = raw[0] + 2.0 * sum(raw[1:])
    return [value / whole for value in raw]


def across_rows(tall, first, count):
    taps = window_taps()
    around = (count + 2) * LANES
    blurred = []
    for f in range(tall.shape[0]):
        given = tall[f, :, LANES * first : LANES * first + around]
        near = [pltpu.roll(given, 1, 1), given, pltpu.roll(given, around - 1, 1), pltpu.roll(given, around - 2, 1)]
        far = []
        for a in range(3):
            total = None
            for b in range(4):
                if 4 * a + b < 11:
                    term = taps[abs(4 * a + b - 5)] * near[b]
                    total = term if total is None else total + term
            far.append(total)
        total = pltpu.roll(far[0], 4, 1) + far[1] + pltpu.roll(far[2], around - 4, 1)
        blurred.append(total[:, LANES : LANES + count * LANES])
    return blurred


def clear_sides(tall):
    blank = jnp.zeros((tall.shape[0], 16, LANES), F32)
    tall[:, :, 0:LANES] = blank
    tall[:, :, tall.shape[2] - LANES :] = blank


def down_columns(fields, f):
    taps = window_taps()
    total = taps[0] * fields[f, 5:21, :]
    for k in range(1, 6):
        total = total + taps[k] * (fields[f, 5 - k : 21 - k, :] + fields[f, 5 + k : 21 + k, :])
    return total


def span(j):
    return pl.ds(pl.multiple_of(LANES * j, LANES), LANES)


RUN = 5


def target_kernel(target_ref, up_ref, down_ref, out_ref, fields, tall):
    spans = target_ref.shape[3] // LANES
    clear_sides(tall)

    @pl.loop(0, 3)
    def _(c):
        @pl.loop(0, spans)
        def _(j):
            fields[0, 0:5, :] = up_ref[c, :, span(j)]
            fields[0, 5:21, :] = target_ref[0, c, :, span(j)]
            fields[0, 21:26, :] = down_ref[c, :, span(j)]
            fields[1] = fields[0] * fields[0]
            for f in range(2):
                tall[f, :, span(j + 1)] = down_columns(fields, f)

        for first in range(0, spans, RUN):
            count = min(RUN, spans - first)
            for f, value in enumerate(across_rows(tall, first, count)):
                out_ref[f, c, :, LANES * first : LANES * (first + count)] = value


def own_kernel(image_ref, target_ref, out_ref, fields, tall):
    spans = target_ref.shape[3] // LANES
    clear_sides(tall)
    fields[...] = jnp.zeros(fields.shape, F32)

    @pl.loop(0, 3)
    def _(c):
        @pl.loop(0, spans)
        def _(j):
            x = image_ref[0, c, :, span(j)]
            y = target_ref[0, c, :, span(j)]
            fields[0, 5:21, :] = x
            fields[1, 5:21, :] = x * x
            fields[2, 5:21, :] = x * y
            for f in range(3):
                tall[f, :, span(j + 1)] = down_columns(fields, f)

        for first in range(0, spans, RUN):
            count = min(RUN, spans - first)
            for f, value in enumerate(across_rows(tall, first, count)):
                out_ref[f, c, :, LANES * first : LANES * (first + count)] = value


def loss_kernel(
    image_ref, target_ref, own_ref, fixed_ref, up_ref, down_ref, target_up, target_down,
    image_out, loss_ref, fields, tall,
):
    taps = window_taps()
    image_out[...] = image_ref[...]
    spans = image_ref.shape[3] // LANES
    clear_sides(tall)
    fields[...] = jnp.zeros(fields.shape, F32)

    @pl.loop(0, 3)
    def _(c):
        @pl.loop(0, spans)
        def _(j):
            x = up_ref[c, :, span(j)]
            y = target_up[c, :, span(j)]
            for f, value in enumerate((x, x * x, x * y)):
                fields[f, 3:8, :] = value
            x = down_ref[c, :, span(j)]
            y = target_down[c, :, span(j)]
            for f, value in enumerate((x, x * x, x * y)):
                fields[f, 24:29, :] = value
            for f in range(3):
                above = taps[1] * fields[f, 7:15, :]
                below = taps[1] * fields[f, 17:25, :]
                for k in range(2, 6):
                    above = above + taps[k] * fields[f, 8 - k : 16 - k, :]
                    below = below + taps[k] * fields[f, 16 + k : 24 + k, :]
                tall[f, 0:8, span(j + 1)] = above
                tall[f, 8:16, span(j + 1)] = below

        for first in range(0, spans, RUN):
            count = min(RUN, spans - first)
            lanes = slice(LANES * first, LANES * (first + count))
            mx, xx, xy = [
                value + own_ref[f, c, :, lanes]
                for f, value in enumerate(across_rows(tall, first, count))
            ]
            my = fixed_ref[0, c, :, lanes]
            both = mx * my
            sums = mx * mx + my * my
            ssim = (2.0 * both + 0.0001) * (2.0 * (xy - both) + 0.0009) / (
                (sums + 0.0001) * (xx + fixed_ref[1, c, :, lanes] - sums + 0.0009)
            )
            gap = jnp.abs(image_ref[0, c, :, lanes] - target_ref[0, c, :, lanes])
            part = (0.8 / 3.0) * gap - (0.2 / 3.0) * ssim
            loss_ref[0, :, lanes] = jnp.where(c == 0, 0.2, loss_ref[0, :, lanes]) + part


def call(kernel, outs, specs, scratch=(), mem=8, work=0):
    return pl.pallas_call(
        kernel,
        out_shape=outs,
        in_specs=[pl.BlockSpec(memory_space=spec) for spec in specs],
        scratch_shapes=list(scratch),
        cost_estimate=pl.CostEstimate(flops=work, bytes_accessed=0, transcendentals=0) if work else None,
        compiler_params=pltpu.CompilerParams(vmem_limit_bytes=mem * 2**20),
    )


def local(gauss_params, visible, cameras, tile_ids, tile_blocks, target):
    cells = lax.axis_size("cell")
    groups = lax.axis_size("view")
    devices = cells * groups
    half = cells // 2
    quarter = cells // 4
    blocks = gauss_params.shape[1] // GBLK
    cap = -(-blocks // devices)
    width = target.shape[3]
    per_row = width // 16
    tiles = tile_ids.shape[2]
    rcap = -(-tiles // cells)
    length = tile_blocks.shape[3]
    rows = LANES + 32
    shape = jax.ShapeDtypeStruct
    my_cell = lax.axis_index("cell").astype(jnp.int32)
    my_view = lax.axis_index("view").astype(jnp.int32)
    me = jnp.stack([my_cell * groups + my_view, my_cell, my_view])
    down_pairs = [(s, (s + 1) % cells) for s in range(cells) if (s - quarter) % half != half - 1]
    up_pairs = [(b, a) for a, b in down_pairs]
    lists = jnp.swapaxes(tile_blocks[0, 0], 0, 1)
    own_table = jnp.concatenate([lists, tile_ids[0]], axis=0)
    table = lax.all_to_all(
        jnp.broadcast_to(own_table, (devices, length + 1, tiles)),
        ("cell", "view"), split_axis=0, concat_axis=0, tiled=True,
    )
    work = blocks * GBLK * 10000
    feats, route = call(
        functools.partial(prepare_kernel, cells, groups, cap, rcap, per_row),
        (shape((visible.shape[0], 9, rows, GBLK), F32), shape((8, LANES), jnp.int32)),
        [SMEM, VMEM, HBM, HBM],
        [
            VMEM((LANES, LANES), F32),
            VMEM((512, LANES), F32),
            VMEM((64, LANES), jnp.int32),
            VMEM(gauss_params.shape, F32),
            VMEM(visible.shape, jnp.int32),
            pltpu.SemaphoreType.DMA((PIECES + 1,)),
        ],
        50, work,
    )(cameras, own_table, gauss_params, visible)
    edge = shape((3, 5, width), F32)
    made, code, target_head, target_tail = call(
        functools.partial(render_kernel, cells, groups, cap, rcap, per_row, blocks),
        (shape((devices, 8 * cap, LANES), F32), shape((devices, LANES), jnp.int32), edge, edge),
        [SMEM, VMEM, VMEM, VMEM],
        [
            VMEM((length + 1, devices, LANES), F32),
            VMEM((2 * LANES, LANES), F32),
            VMEM((2, 9, LANES, LANES), F32),
            VMEM((1024, LANES), F32),
            VMEM((256, LANES), F32),
            VMEM((rows * 8, LANES), F32),
            VMEM((devices, LANES), jnp.int32),
            SMEM((devices, LANES), jnp.int32),
            pltpu.SemaphoreType.DMA,
        ],
        12, work,
    )(me, table, feats, target)
    target_up = lax.ppermute(target_tail, "cell", down_pairs)
    target_down = lax.ppermute(target_head, "cell", up_pairs)
    got = lax.all_to_all(made, ("cell", "view"), split_axis=0, concat_axis=0, tiled=True)
    planes = shape((1, 3, 16, width), F32)
    fixed = call(
        target_kernel,
        shape((2, 3, 16, width), F32),
        [VMEM] * 3,
        [VMEM((2, 32, LANES), F32), VMEM((2, 16, width + 2 * LANES), F32)],
        8, work,
    )(target, target_up, target_down)
    tile_rows = call(
        functools.partial(combine_kernel, tiles),
        shape((cells * 6 * rcap, LANES), F32),
        [SMEM, VMEM, pl.ANY],
    )(route, got.reshape(devices * cap * 8, LANES), fixed)
    got_tiles = lax.all_to_all(
        tile_rows.reshape(cells, 6 * rcap, LANES), "cell", split_axis=0, concat_axis=0, tiled=True
    )
    image, head, tail = call(
        functools.partial(place_kernel, groups, cap, rcap, per_row),
        (planes, edge, edge),
        [SMEM, SMEM, VMEM],
        [VMEM((8 * (per_row + 1), LANES), F32)],
    )(code, me, got_tiles)
    up_rows = lax.ppermute(tail, "cell", down_pairs)
    down_rows = lax.ppermute(head, "cell", up_pairs)
    blur_room = [VMEM((3, 32, LANES), F32), VMEM((3, 16, width + 2 * LANES), F32)]
    own = call(
        own_kernel, shape((3, 3, 16, width), F32), [VMEM] * 2, blur_room, 8, work
    )(image, target)
    return call(
        loss_kernel, (planes, shape((1, 16, width), F32)), [VMEM] * 8, blur_room, 8
    )(image, target, own, fixed, up_rows, down_rows, target_up, target_down)


def solution(mesh):
    return jax.shard_map(
        local,
        mesh=mesh,
        in_specs=(
            P(None, ("cell", "view")),
            P(None, ("cell", "view")),
            P(),
            P("cell", "view", None),
            P("cell", "view", None, None),
            P("view", None, "cell", None),
        ),
        out_specs=(P("view", None, "cell", None), P("view", "cell", None)),
        check_vma=False,
    )
```

```python
import functools
import math

import jax
import jax.numpy as jnp
from jax import lax
from jax.experimental import pallas as pl
from jax.experimental.pallas import tpu as pltpu
from jax.sharding import PartitionSpec as P

GBLK = 128
LANES = 128
LOG2E = math.log2(math.e)
VMEM = pltpu.VMEM
SMEM = pltpu.SMEM
HBM = pltpu.HBM
PIECES = 4
F32 = jnp.float32


def iota(shape, dim):
    return lax.broadcasted_iota(jnp.int32, shape, dim)


def split(value, size):
    whole = jnp.floor((value + 0.5) * (1.0 / size))
    return whole, value - whole * size


def route_kernel(
    cells, blocks, cap, rcap, per_row, me_ref, table_ref, all_ref, late_ref, route_ref, code_ref, box, ids
):
    del late_ref
    length, tiles = table_ref.shape[0] - 1, table_ref.shape[1]
    box[...] = jnp.full(box.shape, -1.0, F32)
    box[0 : length + 1, 0:tiles] = table_ref[...].astype(F32)
    rows = box[...]
    columns = rows.T
    earlier = iota((LANES, LANES), 1) < iota((LANES, LANES), 0)

    def count(mask):
        return jnp.sum(jnp.where(mask, 1.0, 0.0), axis=1, keepdims=True)

    stripe, _ = split(columns[:, length : length + 1], per_row)
    stripe_row, _ = split(rows[length : length + 1, :], per_row)
    tile_rank = count((stripe == stripe_row) & earlier)
    owner_rows = [split(rows[n : n + 1, :], blocks)[0] for n in range(length)]
    values = []
    for n in range(length):
        entry = columns[:, n : n + 1]
        owner, _ = split(entry, blocks)
        rank = count((owner == owner_rows[n]) & earlier)
        for m in range(n):
            rank = rank + count(owner == owner_rows[m])
        values.append(jnp.where(entry >= 0.0, owner * cap + rank, -1.0))
    message = 10 * rcap
    lower = jnp.where(stripe + 1.0 < cells, stripe + 1.0, 0.0)
    upper = jnp.where(stripe > 0.0, stripe - 1.0, cells - 1.0)
    values.append(stripe * message + 6 * tile_rank)
    values.append(lower * message + 6 * rcap + 2 * tile_rank)
    values.append(upper * message + 8 * rcap + 2 * tile_rank)
    lane = iota((LANES, LANES), 1)
    route = jnp.zeros((LANES, LANES), F32)
    for number, value in enumerate(values):
        route = jnp.where(lane == number, value, route)
    route_ref[...] = route.T[0:8, :].astype(jnp.int32)

    devices = all_ref.shape[0]
    ids[...] = jnp.full(ids.shape, -1.0, F32)
    ids[:, 0:tiles] = all_ref[:, length, :].astype(F32)
    stripe, column = split(ids[...], per_row)
    before = jnp.where(iota((LANES, LANES), 0) < iota((LANES, LANES), 1), 1.0, 0.0)
    my_stripe = me_ref[1].astype(F32)
    code_lane = iota((devices, LANES), 1)
    codes = jnp.zeros((devices, LANES), F32)
    lower = jnp.where(my_stripe + 1.0 < cells, my_stripe + 1.0, 0.0)
    upper = jnp.where(my_stripe > 0.0, my_stripe - 1.0, cells - 1.0)
    for number, wanted in enumerate((my_stripe, upper, lower)):
        here = stripe == wanted
        rank = jnp.dot(jnp.where(here, 1.0, 0.0), before, preferred_element_type=F32)
        for k in range(rcap):
            lane = number * rcap + k
            codes = jnp.where(code_lane == lane, jnp.sum(jnp.where(here & (rank == k), column + 1.0, 0.0), axis=1, keepdims=True), codes)
    code_ref[...] = codes.astype(jnp.int32)


def harmonics(x, y, z):
    xx, yy, zz = x * x, y * y, z * z
    return [
        None,
        -0.4886025119029199 * y,
        0.4886025119029199 * z,
        -0.4886025119029199 * x,
        1.0925484305920792 * x * y,
        -1.0925484305920792 * y * z,
        0.31539156525252005 * (2.0 * zz - xx - yy),
        -1.0925484305920792 * x * z,
        0.5462742152960396 * (xx - yy),
        -0.5900435899266435 * y * (3.0 * xx - yy),
        2.890611442640554 * x * y * z,
        -0.4570457994644658 * y * (4.0 * zz - xx - yy),
        0.3731763325901154 * z * (2.0 * zz - 3.0 * xx - 3.0 * yy),
        -0.4570457994644658 * x * (4.0 * zz - xx - yy),
        1.445305721320277 * z * (xx - yy),
        -0.5900435899266435 * x * (xx - 3.0 * yy),
    ]


def view_free(param):
    mean = [param(n) for n in range(3)]
    re, qx, qy, qz = [param(6 + n) for n in range(4)]
    inv_sq = 2.0 / (re * re + qx * qx + qy * qy + qz * qz)
    sqx, sqy, sqz = qx * inv_sq, qy * inv_sq, qz * inv_sq
    xx, yy, zz = qx * sqx, qy * sqy, qz * sqz
    xy, xz, yz = qx * sqy, qx * sqz, qy * sqz
    rx, ry, rz = re * sqx, re * sqy, re * sqz
    turn = [
        [1.0 - (yy + zz), xy - rz, xz + ry],
        [xy + rz, 1.0 - (xx + zz), yz - rx],
        [xz - ry, yz + rx, 1.0 - (xx + yy)],
    ]
    scale = [jnp.exp(2.0 * param(3 + n)) for n in range(3)]
    log_opacity = -LOG2E * jnp.log(1.0 + jnp.exp(-param(10)))
    return mean, turn, scale, log_opacity


def project(param, free, cam, seen):
    mean, turn, scale, log_opacity = free
    rot = [[cam(3 * i + j) for j in range(3)] for i in range(3)]
    shift = [cam(9 + i) for i in range(3)]
    focal = cam(12)
    pc = [rot[i][0] * mean[0] + rot[i][1] * mean[1] + rot[i][2] * mean[2] + shift[i] for i in range(3)]
    inv_depth = 1.0 / pc[2]
    scaled = focal * inv_depth
    off_x = scaled * pc[0]
    off_y = scaled * pc[1]
    jac_x = off_x * inv_depth
    jac_y = off_y * inv_depth
    with_cam = [
        [scaled * rot[0][j] - jac_x * rot[2][j] for j in range(3)],
        [scaled * rot[1][j] - jac_y * rot[2][j] for j in range(3)],
    ]
    whole = [
        [sum(with_cam[i][m] * turn[m][j] for m in range(3)) for j in range(3)] for i in range(2)
    ]
    heavy = [[scale[j] * whole[i][j] for j in range(3)] for i in range(2)]
    cov_a = heavy[0][0] * whole[0][0] + heavy[0][1] * whole[0][1] + heavy[0][2] * whole[0][2] + 0.3
    cov_b = heavy[0][0] * whole[1][0] + heavy[0][1] * whole[1][1] + heavy[0][2] * whole[1][2]
    cov_c = heavy[1][0] * whole[1][0] + heavy[1][1] * whole[1][1] + heavy[1][2] * whole[1][2] + 0.3
    inv_det = LOG2E / (cov_a * cov_c - cov_b * cov_b)
    eye = [rot[0][j] * shift[0] + rot[1][j] * shift[1] + rot[2][j] * shift[2] for j in range(3)]
    head = [mean[j] + eye[j] for j in range(3)]
    inv_dist = lax.rsqrt(head[0] * head[0] + head[1] * head[1] + head[2] * head[2])
    basis = harmonics(*[part * inv_dist for part in head])
    colours = []
    for channel in range(3):
        total = 0.5 + 0.28209479177387814 * param(11 + channel)
        for j in range(1, 16):
            total = total + basis[j] * param(11 + 3 * j + channel)
        colours.append(jnp.maximum(total, 0.0))
    return [
        off_x + cam(13),
        off_y + cam(14),
        -0.5 * cov_c * inv_det,
        cov_b * inv_det,
        -0.5 * cov_a * inv_det,
        jnp.where(seen > 0, log_opacity, -1e30),
    ] + colours


def prepare_kernel(
    cams_ref, params_hbm, seen_hbm, feats_ref,
    stage, seen_stage, params_ref, seen_ref, sems,
):
    features, total = params_ref.shape
    blocks = total // GBLK
    views = seen_ref.shape[0]
    seen_copy = pltpu.make_async_copy(seen_hbm, seen_ref, sems.at[PIECES])
    seen_copy.start()
    groups_all = -(-blocks // 8)
    per_piece = -(-groups_all // PIECES)
    copies = []
    for piece in range(PIECES):
        low = piece * per_piece * 8 * GBLK
        lanes = pl.ds(low, min(per_piece * 8 * GBLK, total - low))
        copies.append(
            pltpu.make_async_copy(params_hbm.at[:, lanes], params_ref.at[:, lanes], sems.at[piece])
        )
        copies[-1].start()
    seen_copy.wait()

    def project_group(group):
        first = jnp.minimum(8 * group, blocks - 8)
        for b in range(8):
            lanes = pl.ds(pl.multiple_of((first + b) * GBLK, GBLK), GBLK)
            for i in range(-(-features // 8)):
                high = min(8, features - 8 * i)
                stage[pl.ds((8 * i + b) * 8, high), :] = params_ref[pl.ds(8 * i, high), lanes]
            seen_stage[pl.ds(8 * b, views), :] = seen_ref[:, lanes]

        def param(r):
            return stage[pl.ds((r // 8) * 64 + r % 8, 8, stride=8), :]

        free = view_free(param)
        for view in range(views):
            seen = seen_stage[pl.ds(view, 8, stride=8), :]
            made = project(param, free, lambda number: cams_ref[view, number], seen)
            for number, value in enumerate(made):
                feats_ref[view, number, pl.ds(first, 8), :] = value

    for piece in range(PIECES):
        copies[piece].wait()
        pl.loop(piece * per_piece, min((piece + 1) * per_piece, groups_all))(project_group)


def render_kernel(
    cells, groups, cap, per_row, blocks,
    me_ref, table_ref, feats_ref, target_ref, out_hbm, head_hbm, tail_hbm,
    box, info, turned, shades, rest, sheets, code_box, code_smem, out_ref, edges, sems,
):
    edges[0] = target_ref[0, :, 0:5, :]
    edges[1] = target_ref[0, :, 11:16, :]
    outward = [
        pltpu.make_async_copy(edges.at[0], head_hbm, sems.at[1]),
        pltpu.make_async_copy(edges.at[1], tail_hbm, sems.at[2]),
        pltpu.make_async_copy(out_ref, out_hbm, sems.at[3]),
    ]
    outward[0].start()
    outward[1].start()
    devices = cells * groups
    quarter, half = cells // 4, cells // 2
    length, tiles = table_ref.shape[1] - 1, table_ref.shape[2]
    views = feats_ref.shape[0]
    box[...] = jnp.full(box.shape, -1.0, F32)
    for n in range(length + 1):
        box[n, :, 0:tiles] = table_ref[:, n, :].astype(F32)
    me = me_ref[0].astype(F32)
    before = jnp.where(iota((LANES, LANES), 0) < iota((LANES, LANES), 1), 1.0, 0.0)

    def ranks(mask):
        ones = jnp.where(mask, 1.0, 0.0)
        return jnp.dot(ones, before, preferred_element_type=F32), jnp.sum(ones, axis=1, keepdims=True)

    def pick(mask, value):
        return jnp.sum(jnp.where(mask, value, 0.0), axis=1, keepdims=True)

    stripe, column = split(box[length], per_row)
    shifted = stripe - quarter
    shifted = jnp.where(shifted < 0.0, shifted + cells, shifted)
    group_of = jnp.bitwise_and(iota((devices, 1), 0), groups - 1).astype(F32)
    tile_code = column + 128.0 * shifted + 16384.0 * group_of
    code_lane = iota((devices, LANES), 1)
    codes = jnp.zeros((devices, LANES), F32)
    prior = jnp.zeros((devices, 1), F32)
    mine = []
    for n in range(length):
        owner, local_slot = split(box[n], blocks)
        hit = owner == me
        rank, total = ranks(hit)
        mine.append((hit, rank + prior, local_slot))
        prior = prior + total
    slot_lane = iota((devices, 2 * LANES), 1).astype(F32)
    found = jnp.zeros((1, 2 * LANES), F32)
    for k in range(cap):
        asked = sum(pick(hit & (rank == k), local_slot + 1.0) for hit, rank, local_slot in mine)
        tile = sum(pick(hit & (rank == k), tile_code) for hit, rank, local_slot in mine)
        codes = jnp.where(code_lane == k, asked, codes)
        found = found + jnp.sum(jnp.where(slot_lane == asked - 1.0, tile, 0.0), axis=0, keepdims=True)
    code_box[...] = codes.astype(jnp.int32)
    scalars = pltpu.make_async_copy(code_box, code_smem, sems.at[0])
    scalars.start()

    for part in range(2):
        row = found[:, part * LANES : (part + 1) * LANES]
        info[pl.ds(part * LANES, LANES), :] = jnp.broadcast_to(row, (LANES, LANES)).T
    for part in range(2):
        count = (LANES, 32)[part]
        rows = pl.ds(part * LANES, count)
        tile = info[rows, :].astype(jnp.int32)
        column = jnp.bitwise_and(tile, 127)
        shifted = jnp.bitwise_and(tile >> 7, 127)
        side = (shifted >= half).astype(jnp.int32)
        view = 2 * (tile >> 14) + side
        anchors = [(16 * column).astype(F32), (16 * (shifted - side * half)).astype(F32)]
        is_view = [view == w for w in range(1, views)]
        for number in range(9):
            value = feats_ref[0, number, rows, :]
            for w in range(1, views):
                value = jnp.where(is_view[w - 1], feats_ref[w, number, rows, :], value)
            if number < 2:
                value = value - anchors[number]
            if part == 1:
                value = jnp.concatenate([value] * 4, axis=0)
            turned[part, number] = value.T

    across = [iota((8, LANES), 0).astype(F32) + 8.0 * xh for xh in range(2)]
    unroll = 4

    def composite(part, pixel_rows):
        def steps(n, carry):
            trans = list(carry[0])
            colour = [list(rows) for rows in carry[1]]
            for u in range(unroll):
                sx, sy, ca, cb, cc, lo, *shade = [
                    jnp.broadcast_to(turned[part, f, pl.ds(unroll * n + u, 1), :], (8, LANES))
                    for f in range(9)
                ]
                dx = [across[xh] - sx for xh in range(2)]
                flat = [ca * dx[xh] * dx[xh] + lo for xh in range(2)]
                mixed = [cb * dx[xh] for xh in range(2)]
                for yl in range(4):
                    dy = pixel_rows[yl] - sy
                    bend = cc * dy
                    for xh in range(2):
                        v = 2 * yl + xh
                        weight = jnp.exp2(flat[xh] + dy * (mixed[xh] + bend)) * trans[v]
                        trans[v] = trans[v] - weight
                        for c in range(3):
                            colour[c][v] = colour[c][v] + weight * shade[c]
            return tuple(trans), tuple(tuple(rows) for rows in colour)

        zero = jnp.zeros((8, LANES), F32)
        start = (tuple(zero + 1.0 for _ in range(8)), tuple(tuple(zero for _ in range(8)) for _ in range(3)))
        trans, colour = lax.fori_loop(0, GBLK // unroll, steps, start)
        return [*colour, trans]

    @pl.loop(0, 4)
    def _(chunk):
        high, odd = chunk >> 1, jnp.bitwise_and(chunk, 1)
        pixel_rows = [
            (8 * high + jnp.bitwise_and(8 - 4 * odd - yl, 7)).astype(F32) for yl in range(4)
        ]
        planes = composite(0, pixel_rows)
        for c in range(4):
            for v in range(8):
                shades[pl.ds(c * 256 + chunk * 64 + 8 * v, 8), :] = planes[c][v]

    chunk = iota((8, LANES), 1) >> 5
    high, odd = chunk >> 1, jnp.bitwise_and(chunk, 1)
    pixel_rows = [
        (8 * high + jnp.bitwise_and(8 - 4 * odd - yl, 7)).astype(F32) for yl in range(4)
    ]
    planes = composite(1, pixel_rows)
    for c in range(4):
        for v in range(8):
            rest[pl.ds(c * 64 + 8 * v, 8), :] = planes[c][v]

    for r in range(8):
        sheets[pl.ds(r, LANES, stride=8), :] = shades[pl.ds(r * LANES, LANES), :].T
    left = iota((32, LANES), 1) < 64
    for pair in range(2):
        both = rest[pl.ds(pair * LANES, LANES), :].T
        parts = [both[32 * q : 32 * q + 32, :] for q in range(4)]
        swapped = [pltpu.roll(part, 64, 1) for part in parts]
        for h in range(2):
            low = jnp.where(left, parts[2 * h], swapped[2 * h + 1])
            high = jnp.where(left, swapped[2 * h], parts[2 * h + 1])
            sheets[pl.ds(LANES * 8 + 4 * pair + h, 32, stride=8), :] = low
            sheets[pl.ds(LANES * 8 + 4 * pair + 2 + h, 32, stride=8), :] = high
    scalars.wait()

    @pl.loop(0, devices)
    def _(d):
        for k in range(cap):
            place = jnp.clip(code_smem[d, k] - 1, 0, blocks - 1)
            out_ref[d, pl.ds(8 * k, 8), :] = sheets[pl.ds(pl.multiple_of(8 * place, 8), 8), :]

    outward[2].start()
    for copy in outward:
        copy.wait()


def lane_group(low, high):
    group = iota((8, LANES), 1) >> 4
    return (group >= low) & (group <= high)


def combine_kernel(tiles, route_ref, got_ref, early_up, early_down, out_ref):
    del early_up, early_down
    line = iota((8, LANES), 0)
    from_half = ((line == 0) & lane_group(1, 3)) | ((line == 1) & (lane_group(6, 7) | lane_group(0, 0)))
    from_left = ((line == 2) & lane_group(1, 1)) | ((line == 3) & lane_group(6, 6))
    from_right = ((line == 2) & lane_group(3, 3)) | ((line == 3) & lane_group(0, 0))

    @pl.loop(0, tiles, unroll=8)
    def _(t):
        front = route_ref[0, t]
        back = route_ref[1, t]
        near = got_ref[pl.ds(pl.multiple_of(8 * front, 8), 8), :]
        far = got_ref[pl.ds(pl.multiple_of(8 * jnp.maximum(back, 0), 8), 8), :]
        keep = jnp.where(line >= 6, near, 0.0)
        keep = keep + pltpu.roll(keep, 4, 0)
        keep = keep + pltpu.roll(keep, 2, 0)
        tile = near + jnp.where(back >= 0, keep * far, 0.0)
        out_ref[pl.ds(route_ref[2, t], 6), :] = tile[0:6, :]
        two_up = pltpu.roll(tile, 6, 0)
        edge = jnp.where(from_half, pltpu.roll(pltpu.roll(tile, 4, 0), 64, 1), tile)
        edge = jnp.where(from_left, pltpu.roll(two_up, 16, 1), edge)
        edge = jnp.where(from_right, pltpu.roll(two_up, LANES - 16, 1), edge)
        low = route_ref[3, t]
        high = route_ref[4, t]
        out_ref[pl.ds(low, 1), :] = edge[1:2, :]
        out_ref[pl.ds(low + 1, 1), :] = edge[3:4, :]
        out_ref[pl.ds(high, 1), :] = edge[0:1, :]
        out_ref[pl.ds(high + 1, 1), :] = edge[2:3, :]


def window_taps():
    raw = [math.exp(-k * k / 4.5) for k in range(6)]
    whole = raw[0] + 2.0 * sum(raw[1:])
    return [value / whole for value in raw]


def across_rows(tall, rows, first, count):
    taps = window_taps()
    around = (count + 2) * LANES
    blurred = []
    for f in range(tall.shape[0]):
        given = tall[f, rows, LANES * first : LANES * first + around]
        near = [pltpu.roll(given, 1, 1), given, pltpu.roll(given, around - 1, 1), pltpu.roll(given, around - 2, 1)]
        far = []
        for a in range(3):
            total = None
            for b in range(4):
                if 4 * a + b < 11:
                    term = taps[abs(4 * a + b - 5)] * near[b]
                    total = term if total is None else total + term
            far.append(total)
        total = pltpu.roll(far[0], 4, 1) + far[1] + pltpu.roll(far[2], around - 4, 1)
        blurred.append(total[:, LANES : LANES + count * LANES])
    return blurred


def clear_sides(tall):
    blank = jnp.zeros((tall.shape[0], 16, LANES), F32)
    tall[:, :, 0:LANES] = blank
    tall[:, :, tall.shape[2] - LANES :] = blank


def down_columns(fields, u, f):
    taps = window_taps()
    total = taps[0] * fields[u, f, 8:24, :]
    for k in range(1, 6):
        total = total + taps[k] * (fields[u, f, 8 - k : 24 - k, :] + fields[u, f, 8 + k : 24 + k, :])
    return total


def span(j):
    return pl.ds(pl.multiple_of(LANES * j, LANES), LANES)


RUN = 5
HALVES = (slice(0, 8), slice(8, 16))


def target_kernel(target_ref, up_ref, down_ref, late_ref, out_ref, fields, tall):
    del late_ref
    spans = target_ref.shape[3] // LANES
    clear_sides(tall)

    @pl.loop(0, 3)
    def _(c):
        @pl.loop(0, spans // RUN)
        def _(run):
            for u in range(RUN):
                j = RUN * run + u
                for low, high, y in (
                    (3, 8, up_ref[c, :, span(j)]),
                    (8, 24, target_ref[0, c, :, span(j)]),
                    (24, 29, down_ref[c, :, span(j)]),
                ):
                    fields[u, 0, low:high, :] = y
                    fields[u, 1, low:high, :] = y * y
            for u in range(RUN):
                for f in range(2):
                    tall[f, :, span(RUN * run + u + 1)] = down_columns(fields, u, f)

        for first in range(0, spans, RUN):
            count = RUN
            for rows in HALVES:
                for f, value in enumerate(across_rows(tall, rows, first, count)):
                    out_ref[f, c, rows, LANES * first : LANES * (first + count)] = value


def finish_kernel(
    groups, rcap, per_row,
    code_ref, me_ref, got_ref, target_ref, fixed_ref, target_up, target_down, image_ref, loss_ref,
    board, edges, halo, fields, tall,
):
    cells = got_ref.shape[0]
    spans = target_ref.shape[3] // LANES

    @pl.loop(0, cells)
    def _(cell):
        line = cell * groups + me_ref[2]

        def spot(k):
            column = code_ref[line, k] - 1
            return jnp.where(column < 0, per_row, column)

        for k in range(rcap):
            board[pl.ds(8 * spot(k), 6), :] = got_ref[cell, 6 * k : 6 * k + 6, :]
        for side in range(2):
            for k in range(rcap):
                first = (6 + 2 * side) * rcap + 2 * k
                edges[side, pl.ds(2 * spot((1 + side) * rcap + k), 2), :] = got_ref[cell, first : first + 2, :]

    masks = [jnp.bitwise_and(iota((8, LANES), 1) >> 4, bit) != 0 for bit in (1, 2, 4)]

    def pixels(made):
        made = pltpu.roll(made, 0, 1, stride=16, stride_axis=0)
        for mask, bit in zip(masks, (1, 2, 4)):
            made = jnp.where(mask, pltpu.roll(made, 8 - bit, 0), made)
        return pltpu.roll(made, 0, 1, stride=16, stride_axis=0)

    for j in range(spans):
        lanes = slice(LANES * j, LANES * j + LANES)
        for c in range(3):
            for h in range(2):
                image_ref[0, c, 8 * h : 8 * h + 8, lanes] = pixels(
                    board[pl.ds(64 * j + 2 * c + h, 8, stride=8), :]
                )
        for side in range(2):
            kept = me_ref[3 + side] > 0
            first = edges[side, pl.ds(16 * j, 8, stride=2), :]
            second = edges[side, pl.ds(16 * j + 1, 8, stride=2), :]
            half = pltpu.roll(first, 64, 1)
            left = pltpu.roll(second, LANES - 16, 1)
            right = pltpu.roll(second, 16, 1)
            if side == 0:
                third = jnp.where(lane_group(2, 4), half, jnp.where(lane_group(1, 1), right, left))
            else:
                third = jnp.where(lane_group(5, 7), half, jnp.where(lane_group(4, 4), right, left))
            for c, value in enumerate((first, second, third)):
                halo[side, c, :, lanes] = jnp.where(kept, pixels(value), 0.0)

    clear_sides(tall)

    @pl.loop(0, 3)
    def _(c):
        @pl.loop(0, spans // RUN)
        def _(run):
            for u in range(RUN):
                j = RUN * run + u
                for low, high, x, y in (
                    (3, 8, halo[0, c, 3:8, span(j)], target_up[c, :, span(j)]),
                    (8, 24, image_ref[0, c, :, span(j)], target_ref[0, c, :, span(j)]),
                    (24, 29, halo[1, c, 0:5, span(j)], target_down[c, :, span(j)]),
                ):
                    fields[u, 0, low:high, :] = x
                    fields[u, 1, low:high, :] = x * x
                    fields[u, 2, low:high, :] = x * y
            for u in range(RUN):
                for f in range(3):
                    tall[f, :, span(RUN * run + u + 1)] = down_columns(fields, u, f)

        for first in range(0, spans, RUN):
            count = RUN
            lanes = slice(LANES * first, LANES * (first + count))
            for rows in HALVES:
                mx, xx, xy = across_rows(tall, rows, first, count)
                my = fixed_ref[0, c, rows, lanes]
                both = mx * my
                sums = mx * mx + my * my
                ssim = (2.0 * both + 0.0001) * (2.0 * (xy - both) + 0.0009) / (
                    (sums + 0.0001) * (xx + fixed_ref[1, c, rows, lanes] - sums + 0.0009)
                )
                gap = jnp.abs(image_ref[0, c, rows, lanes] - target_ref[0, c, rows, lanes])
                part = (0.8 / 3.0) * gap - (0.2 / 3.0) * ssim
                loss_ref[0, rows, lanes] = jnp.where(c == 0, 0.2, loss_ref[0, rows, lanes]) + part


def call(kernel, outs, specs, scratch=(), mem=8, work=0, out_space=VMEM):
    return pl.pallas_call(
        kernel,
        out_shape=outs,
        in_specs=[pl.BlockSpec(memory_space=spec) for spec in specs],
        out_specs=jax.tree.map(lambda _: pl.BlockSpec(memory_space=out_space), outs),
        scratch_shapes=list(scratch),
        cost_estimate=pl.CostEstimate(flops=work, bytes_accessed=0, transcendentals=0) if work else None,
        compiler_params=pltpu.CompilerParams(vmem_limit_bytes=mem * 2**20),
    )


def local(gauss_params, visible, cameras, tile_ids, tile_blocks, target):
    cells = lax.axis_size("cell")
    groups = lax.axis_size("view")
    devices = cells * groups
    half = cells // 2
    quarter = cells // 4
    blocks = gauss_params.shape[1] // GBLK
    cap = -(-blocks // devices)
    width = target.shape[3]
    per_row = width // 16
    tiles = tile_ids.shape[2]
    rcap = -(-tiles // cells)
    length = tile_blocks.shape[3]
    rows = LANES + 32
    shape = jax.ShapeDtypeStruct
    my_cell = lax.axis_index("cell").astype(jnp.int32)
    my_view = lax.axis_index("view").astype(jnp.int32)
    place = (my_cell + (cells - quarter)) % half
    me = jnp.stack(
        [my_cell * groups + my_view, my_cell, my_view]
        + [(place != edge).astype(jnp.int32) for edge in (0, half - 1)]
    )
    down_pairs = [(s, (s + 1) % cells) for s in range(cells) if (s - quarter) % half != half - 1]
    up_pairs = [(b, a) for a, b in down_pairs]
    lists = jnp.swapaxes(tile_blocks[0, 0], 0, 1)
    own_table = jnp.concatenate([lists, tile_ids[0]], axis=0)
    table = lax.all_to_all(
        jnp.broadcast_to(own_table, (devices, length + 1, tiles)),
        ("cell", "view"), split_axis=0, concat_axis=0, tiled=True,
    )
    work = blocks * GBLK * 10000
    feats = call(
        prepare_kernel,
        shape((visible.shape[0], 9, rows, GBLK), F32),
        [SMEM, HBM, HBM],
        [
            VMEM((512, LANES), F32),
            VMEM((64, LANES), jnp.int32),
            VMEM(gauss_params.shape, F32),
            VMEM(visible.shape, jnp.int32),
            pltpu.SemaphoreType.DMA((PIECES + 1,)),
        ],
        50, work,
    )(cameras, gauss_params, visible)
    edge = shape((3, 5, width), F32)
    made, target_head, target_tail = call(
        functools.partial(render_kernel, cells, groups, cap, per_row, blocks),
        (HBM((devices, 8 * cap, LANES), F32), HBM(edge.shape, F32), HBM(edge.shape, F32)),
        [SMEM, VMEM, VMEM, VMEM],
        [
            VMEM((length + 1, devices, LANES), F32),
            VMEM((2 * LANES, LANES), F32),
            VMEM((2, 9, LANES, LANES), F32),
            VMEM((1024, LANES), F32),
            VMEM((256, LANES), F32),
            VMEM((rows * 8, LANES), F32),
            VMEM((devices, LANES), jnp.int32),
            SMEM((devices, LANES), jnp.int32),
            VMEM((devices, 8 * cap, LANES), F32),
            VMEM((2,) + edge.shape, F32),
            pltpu.SemaphoreType.DMA((4,)),
        ],
        12, work, HBM,
    )(me, table, feats, target)
    target_up = lax.ppermute(target_tail, "cell", down_pairs)
    target_down = lax.ppermute(target_head, "cell", up_pairs)
    got = lax.all_to_all(made, ("cell", "view"), split_axis=0, concat_axis=0, tiled=True)
    planes = shape((1, 3, 16, width), F32)
    route, code = call(
        functools.partial(route_kernel, cells, blocks, cap, rcap, per_row),
        (shape((8, LANES), jnp.int32), shape((devices, LANES), jnp.int32)),
        [SMEM, VMEM, VMEM, pl.ANY],
        [VMEM((LANES, LANES), F32), VMEM((devices, LANES), F32)],
        8, work,
    )(me, own_table, table, target_head)
    tile_rows = call(
        functools.partial(combine_kernel, tiles),
        shape((cells * 10 * rcap, LANES), F32),
        [SMEM, VMEM, pl.ANY, pl.ANY],
    )(route, got.reshape(devices * cap * 8, LANES), target_up, target_down)
    got_tiles = lax.all_to_all(
        tile_rows.reshape(cells, 10 * rcap, LANES), "cell", split_axis=0, concat_axis=0, tiled=True
    )
    fixed = call(
        target_kernel,
        shape((2, 3, 16, width), F32),
        [VMEM] * 3 + [pl.ANY],
        [VMEM((RUN, 2, 32, LANES), F32), VMEM((2, 16, width + 2 * LANES), F32)],
        8, work,
    )(target, target_up, target_down, tile_rows)
    return call(
        functools.partial(finish_kernel, groups, rcap, per_row),
        (planes, shape((1, 16, width), F32)),
        [SMEM, SMEM] + [VMEM] * 5,
        [
            VMEM((8 * (per_row + 1), LANES), F32),
            VMEM((2, 2 * (per_row + 4), LANES), F32),
            VMEM((2, 3, 8, width), F32),
            VMEM((RUN, 3, 32, LANES), F32),
            VMEM((3, 16, width + 2 * LANES), F32),
        ],
        8,
    )(code, me, got_tiles, target, fixed, target_up, target_down)


def solution(mesh):
    return jax.shard_map(
        local,
        mesh=mesh,
        in_specs=(
            P(None, ("cell", "view")),
            P(None, ("cell", "view")),
            P(),
            P("cell", "view", None),
            P("cell", "view", None, None),
            P("view", None, "cell", None),
        ),
        out_specs=(P("view", None, "cell", None), P("view", "cell", None)),
        check_vma=False,
    )
```

```python
import functools
import math

import jax
import jax.numpy as jnp
from jax import lax
from jax.experimental import pallas as pl
from jax.experimental.pallas import tpu as pltpu
from jax.sharding import PartitionSpec as P

GBLK = 128
LANES = 128
LOG2E = math.log2(math.e)
VMEM = pltpu.VMEM
SMEM = pltpu.SMEM
HBM = pltpu.HBM
PIECES = 4
F32 = jnp.float32


def iota(shape, dim):
    return lax.broadcasted_iota(jnp.int32, shape, dim)


def split(value, size):
    whole = jnp.floor((value + 0.5) * (1.0 / size))
    return whole, value - whole * size


def route_kernel(
    cells, blocks, cap, rcap, per_row, me_ref, all_ref, late_ref, route_ref, code_ref, box, ids
):
    del late_ref
    length, tiles = all_ref.shape[1] - 1, all_ref.shape[2]
    box[...] = jnp.full(box.shape, -1.0, F32)
    box[0 : length + 1, 0:tiles] = all_ref[me_ref[0]].astype(F32)
    rows = box[...]
    columns = rows.T
    earlier = iota((LANES, LANES), 1) < iota((LANES, LANES), 0)

    def count(mask):
        return jnp.sum(jnp.where(mask, 1.0, 0.0), axis=1, keepdims=True)

    stripe, _ = split(columns[:, length : length + 1], per_row)
    stripe_row, _ = split(rows[length : length + 1, :], per_row)
    tile_rank = count((stripe == stripe_row) & earlier)
    owner_rows = [split(rows[n : n + 1, :], blocks)[0] for n in range(length)]
    values = []
    for n in range(length):
        entry = columns[:, n : n + 1]
        owner, _ = split(entry, blocks)
        rank = count((owner == owner_rows[n]) & earlier)
        for m in range(n):
            rank = rank + count(owner == owner_rows[m])
        values.append(jnp.where(entry >= 0.0, owner * cap + rank, -1.0))
    message = 10 * rcap
    lower = jnp.where(stripe + 1.0 < cells, stripe + 1.0, 0.0)
    upper = jnp.where(stripe > 0.0, stripe - 1.0, cells - 1.0)
    values.append(stripe * message + 6 * tile_rank)
    values.append(lower * message + 6 * rcap + 2 * tile_rank)
    values.append(upper * message + 8 * rcap + 2 * tile_rank)
    lane = iota((LANES, LANES), 1)
    route = jnp.zeros((LANES, LANES), F32)
    for number, value in enumerate(values):
        route = jnp.where(lane == number, value, route)
    route_ref[...] = route.T[0:8, :].astype(jnp.int32)

    devices = all_ref.shape[0]
    ids[...] = jnp.full(ids.shape, -1.0, F32)
    ids[:, 0:tiles] = all_ref[:, length, :].astype(F32)
    stripe, column = split(ids[...], per_row)
    before = jnp.where(iota((LANES, LANES), 0) < iota((LANES, LANES), 1), 1.0, 0.0)
    my_stripe = me_ref[1].astype(F32)
    code_lane = iota((devices, LANES), 1)
    codes = jnp.zeros((devices, LANES), F32)
    lower = jnp.where(my_stripe + 1.0 < cells, my_stripe + 1.0, 0.0)
    upper = jnp.where(my_stripe > 0.0, my_stripe - 1.0, cells - 1.0)
    for number, wanted in enumerate((my_stripe, upper, lower)):
        here = stripe == wanted
        rank = jnp.dot(jnp.where(here, 1.0, 0.0), before, preferred_element_type=F32)
        for k in range(rcap):
            lane = number * rcap + k
            codes = jnp.where(code_lane == lane, jnp.sum(jnp.where(here & (rank == k), column + 1.0, 0.0), axis=1, keepdims=True), codes)
    code_ref[...] = codes.astype(jnp.int32)


def harmonics(x, y, z):
    xx, yy, zz = x * x, y * y, z * z
    return [
        None,
        -0.4886025119029199 * y,
        0.4886025119029199 * z,
        -0.4886025119029199 * x,
        1.0925484305920792 * x * y,
        -1.0925484305920792 * y * z,
        0.31539156525252005 * (2.0 * zz - xx - yy),
        -1.0925484305920792 * x * z,
        0.5462742152960396 * (xx - yy),
        -0.5900435899266435 * y * (3.0 * xx - yy),
        2.890611442640554 * x * y * z,
        -0.4570457994644658 * y * (4.0 * zz - xx - yy),
        0.3731763325901154 * z * (2.0 * zz - 3.0 * xx - 3.0 * yy),
        -0.4570457994644658 * x * (4.0 * zz - xx - yy),
        1.445305721320277 * z * (xx - yy),
        -0.5900435899266435 * x * (xx - 3.0 * yy),
    ]


def view_free(param):
    mean = [param(n) for n in range(3)]
    re, qx, qy, qz = [param(6 + n) for n in range(4)]
    inv_sq = 2.0 / (re * re + qx * qx + qy * qy + qz * qz)
    sqx, sqy, sqz = qx * inv_sq, qy * inv_sq, qz * inv_sq
    xx, yy, zz = qx * sqx, qy * sqy, qz * sqz
    xy, xz, yz = qx * sqy, qx * sqz, qy * sqz
    rx, ry, rz = re * sqx, re * sqy, re * sqz
    turn = [
        [1.0 - (yy + zz), xy - rz, xz + ry],
        [xy + rz, 1.0 - (xx + zz), yz - rx],
        [xz - ry, yz + rx, 1.0 - (xx + yy)],
    ]
    scale = [jnp.exp(2.0 * param(3 + n)) for n in range(3)]
    log_opacity = -LOG2E * jnp.log(1.0 + jnp.exp(-param(10)))
    return mean, turn, scale, log_opacity


def project(param, free, cam, seen):
    mean, turn, scale, log_opacity = free
    rot = [[cam(3 * i + j) for j in range(3)] for i in range(3)]
    shift = [cam(9 + i) for i in range(3)]
    focal = cam(12)
    pc = [rot[i][0] * mean[0] + rot[i][1] * mean[1] + rot[i][2] * mean[2] + shift[i] for i in range(3)]
    inv_depth = 1.0 / pc[2]
    scaled = focal * inv_depth
    off_x = scaled * pc[0]
    off_y = scaled * pc[1]
    jac_x = off_x * inv_depth
    jac_y = off_y * inv_depth
    with_cam = [
        [scaled * rot[0][j] - jac_x * rot[2][j] for j in range(3)],
        [scaled * rot[1][j] - jac_y * rot[2][j] for j in range(3)],
    ]
    whole = [
        [sum(with_cam[i][m] * turn[m][j] for m in range(3)) for j in range(3)] for i in range(2)
    ]
    heavy = [[scale[j] * whole[i][j] for j in range(3)] for i in range(2)]
    cov_a = heavy[0][0] * whole[0][0] + heavy[0][1] * whole[0][1] + heavy[0][2] * whole[0][2] + 0.3
    cov_b = heavy[0][0] * whole[1][0] + heavy[0][1] * whole[1][1] + heavy[0][2] * whole[1][2]
    cov_c = heavy[1][0] * whole[1][0] + heavy[1][1] * whole[1][1] + heavy[1][2] * whole[1][2] + 0.3
    inv_det = LOG2E / (cov_a * cov_c - cov_b * cov_b)
    eye = [rot[0][j] * shift[0] + rot[1][j] * shift[1] + rot[2][j] * shift[2] for j in range(3)]
    head = [mean[j] + eye[j] for j in range(3)]
    inv_dist = lax.rsqrt(head[0] * head[0] + head[1] * head[1] + head[2] * head[2])
    basis = harmonics(*[part * inv_dist for part in head])
    colours = []
    for channel in range(3):
        total = 0.5 + 0.28209479177387814 * param(11 + channel)
        for j in range(1, 16):
            total = total + basis[j] * param(11 + 3 * j + channel)
        colours.append(jnp.maximum(total, 0.0))
    return [
        off_x + cam(13),
        off_y + cam(14),
        -0.5 * cov_c * inv_det,
        cov_b * inv_det,
        -0.5 * cov_a * inv_det,
        jnp.where(seen > 0, log_opacity, -1e30),
    ] + colours


def prepare_kernel(
    cams_ref, params_hbm, seen_hbm, feats_ref,
    stage, seen_stage, params_ref, seen_ref, sems,
):
    features, total = params_ref.shape
    blocks = total // GBLK
    views = seen_ref.shape[0]
    seen_copy = pltpu.make_async_copy(seen_hbm, seen_ref, sems.at[PIECES])
    seen_copy.start()
    groups_all = -(-blocks // 8)
    per_piece = -(-groups_all // PIECES)
    copies = []
    for piece in range(PIECES):
        low = piece * per_piece * 8 * GBLK
        lanes = pl.ds(low, min(per_piece * 8 * GBLK, total - low))
        copies.append(
            pltpu.make_async_copy(params_hbm.at[:, lanes], params_ref.at[:, lanes], sems.at[piece])
        )
        copies[-1].start()
    seen_copy.wait()

    def project_group(group):
        first = jnp.minimum(8 * group, blocks - 8)
        for b in range(8):
            lanes = pl.ds(pl.multiple_of((first + b) * GBLK, GBLK), GBLK)
            for i in range(-(-features // 8)):
                high = min(8, features - 8 * i)
                stage[pl.ds((8 * i + b) * 8, high), :] = params_ref[pl.ds(8 * i, high), lanes]
            seen_stage[pl.ds(8 * b, views), :] = seen_ref[:, lanes]

        def param(r):
            return stage[pl.ds((r // 8) * 64 + r % 8, 8, stride=8), :]

        free = view_free(param)
        for view in range(views):
            seen = seen_stage[pl.ds(view, 8, stride=8), :]
            made = project(param, free, lambda number: cams_ref[view, number], seen)
            for number, value in enumerate(made):
                feats_ref[view, number, pl.ds(first, 8), :] = value

    for piece in range(PIECES):
        copies[piece].wait()
        pl.loop(piece * per_piece, min((piece + 1) * per_piece, groups_all))(project_group)


def render_kernel(
    cells, groups, cap, per_row, blocks,
    me_ref, table_ref, feats_ref, target_ref, out_hbm, head_hbm, tail_hbm,
    box, info, turned, shades, rest, sheets, code_box, code_smem, out_ref, edges, sems,
):
    edges[0] = target_ref[0, :, 0:5, :]
    edges[1] = target_ref[0, :, 11:16, :]
    outward = [
        pltpu.make_async_copy(edges.at[0], head_hbm, sems.at[1]),
        pltpu.make_async_copy(edges.at[1], tail_hbm, sems.at[2]),
        pltpu.make_async_copy(out_ref, out_hbm, sems.at[3]),
    ]
    outward[0].start()
    outward[1].start()
    devices = cells * groups
    quarter, half = cells // 4, cells // 2
    length, tiles = table_ref.shape[1] - 1, table_ref.shape[2]
    views = feats_ref.shape[0]
    box[...] = jnp.full(box.shape, -1.0, F32)
    for n in range(length + 1):
        box[n, :, 0:tiles] = table_ref[:, n, :].astype(F32)
    me = me_ref[0].astype(F32)
    before = jnp.where(iota((LANES, LANES), 0) < iota((LANES, LANES), 1), 1.0, 0.0)

    def ranks(mask):
        ones = jnp.where(mask, 1.0, 0.0)
        return jnp.dot(ones, before, preferred_element_type=F32), jnp.sum(ones, axis=1, keepdims=True)

    def pick(mask, value):
        return jnp.sum(jnp.where(mask, value, 0.0), axis=1, keepdims=True)

    stripe, column = split(box[length], per_row)
    shifted = stripe - quarter
    shifted = jnp.where(shifted < 0.0, shifted + cells, shifted)
    group_of = jnp.bitwise_and(iota((devices, 1), 0), groups - 1).astype(F32)
    tile_code = column + 128.0 * shifted + 16384.0 * group_of
    code_lane = iota((devices, LANES), 1)
    codes = jnp.zeros((devices, LANES), F32)
    prior = jnp.zeros((devices, 1), F32)
    mine = []
    for n in range(length):
        owner, local_slot = split(box[n], blocks)
        hit = owner == me
        rank, total = ranks(hit)
        mine.append((hit, rank + prior, local_slot))
        prior = prior + total
    slot_lane = iota((devices, 2 * LANES), 1).astype(F32)
    found = jnp.zeros((1, 2 * LANES), F32)
    for k in range(cap):
        asked = sum(pick(hit & (rank == k), local_slot + 1.0) for hit, rank, local_slot in mine)
        tile = sum(pick(hit & (rank == k), tile_code) for hit, rank, local_slot in mine)
        codes = jnp.where(code_lane == k, asked, codes)
        found = found + jnp.sum(jnp.where(slot_lane == asked - 1.0, tile, 0.0), axis=0, keepdims=True)
    code_box[...] = codes.astype(jnp.int32)
    scalars = pltpu.make_async_copy(code_box, code_smem, sems.at[0])
    scalars.start()

    for part in range(2):
        row = found[:, part * LANES : (part + 1) * LANES]
        info[pl.ds(part * LANES, LANES), :] = jnp.broadcast_to(row, (LANES, LANES)).T
    for part in range(2):
        count = (LANES, 32)[part]
        rows = pl.ds(part * LANES, count)
        tile = info[rows, :].astype(jnp.int32)
        column = jnp.bitwise_and(tile, 127)
        shifted = jnp.bitwise_and(tile >> 7, 127)
        side = (shifted >= half).astype(jnp.int32)
        view = 2 * (tile >> 14) + side
        anchors = [(16 * column).astype(F32), (16 * (shifted - side * half)).astype(F32)]
        is_view = [view == w for w in range(1, views)]
        for number in range(9):
            value = feats_ref[0, number, rows, :]
            for w in range(1, views):
                value = jnp.where(is_view[w - 1], feats_ref[w, number, rows, :], value)
            if number < 2:
                value = value - anchors[number]
            if part == 1:
                value = jnp.concatenate([value] * 4, axis=0)
            turned[part, number] = value.T

    across = [iota((8, LANES), 0).astype(F32) + 8.0 * xh for xh in range(2)]
    unroll = 8

    def composite(part, pixel_rows):
        def steps(n, carry):
            trans = list(carry[0])
            colour = [list(rows) for rows in carry[1]]
            for u in range(unroll):
                sx, sy, ca, cb, cc, lo, *shade = [
                    jnp.broadcast_to(turned[part, f, pl.ds(unroll * n + u, 1), :], (8, LANES))
                    for f in range(9)
                ]
                dx = [across[xh] - sx for xh in range(2)]
                flat = [ca * dx[xh] * dx[xh] + lo for xh in range(2)]
                mixed = [cb * dx[xh] for xh in range(2)]
                for yl in range(4):
                    dy = pixel_rows[yl] - sy
                    bend = cc * dy
                    for xh in range(2):
                        v = 2 * yl + xh
                        weight = jnp.exp2(flat[xh] + dy * (mixed[xh] + bend)) * trans[v]
                        trans[v] = trans[v] - weight
                        for c in range(3):
                            colour[c][v] = colour[c][v] + weight * shade[c]
            return tuple(trans), tuple(tuple(rows) for rows in colour)

        zero = jnp.zeros((8, LANES), F32)
        start = (tuple(zero + 1.0 for _ in range(8)), tuple(tuple(zero for _ in range(8)) for _ in range(3)))
        trans, colour = lax.fori_loop(0, GBLK // unroll, steps, start)
        return [*colour, trans]

    @pl.loop(0, 4)
    def _(chunk):
        high, odd = chunk >> 1, jnp.bitwise_and(chunk, 1)
        pixel_rows = [
            (8 * high + jnp.bitwise_and(8 - 4 * odd - yl, 7)).astype(F32) for yl in range(4)
        ]
        planes = composite(0, pixel_rows)
        for c in range(4):
            for v in range(8):
                shades[pl.ds(c * 256 + chunk * 64 + 8 * v, 8), :] = planes[c][v]

    chunk = iota((8, LANES), 1) >> 5
    high, odd = chunk >> 1, jnp.bitwise_and(chunk, 1)
    pixel_rows = [
        (8 * high + jnp.bitwise_and(8 - 4 * odd - yl, 7)).astype(F32) for yl in range(4)
    ]
    planes = composite(1, pixel_rows)
    for c in range(4):
        for v in range(8):
            rest[pl.ds(c * 64 + 8 * v, 8), :] = planes[c][v]

    for r in range(8):
        sheets[pl.ds(r, LANES, stride=8), :] = shades[pl.ds(r * LANES, LANES), :].T
    left = iota((32, LANES), 1) < 64
    for pair in range(2):
        both = rest[pl.ds(pair * LANES, LANES), :].T
        parts = [both[32 * q : 32 * q + 32, :] for q in range(4)]
        swapped = [pltpu.roll(part, 64, 1) for part in parts]
        for h in range(2):
            low = jnp.where(left, parts[2 * h], swapped[2 * h + 1])
            high = jnp.where(left, swapped[2 * h], parts[2 * h + 1])
            sheets[pl.ds(LANES * 8 + 4 * pair + h, 32, stride=8), :] = low
            sheets[pl.ds(LANES * 8 + 4 * pair + 2 + h, 32, stride=8), :] = high
    scalars.wait()

    @pl.loop(0, devices)
    def _(d):
        for k in range(cap):
            place = jnp.clip(code_smem[d, k] - 1, 0, blocks - 1)
            out_ref[d, pl.ds(8 * k, 8), :] = sheets[pl.ds(pl.multiple_of(8 * place, 8), 8), :]

    outward[2].start()
    for copy in outward:
        copy.wait()


def lane_group(low, high):
    group = iota((8, LANES), 1) >> 4
    return (group >= low) & (group <= high)


def combine_kernel(tiles, route_ref, got_ref, early_up, early_down, out_ref):
    del early_up, early_down
    line = iota((8, LANES), 0)
    from_half = ((line == 0) & lane_group(1, 3)) | ((line == 1) & (lane_group(6, 7) | lane_group(0, 0)))
    from_left = ((line == 2) & lane_group(1, 1)) | ((line == 3) & lane_group(6, 6))
    from_right = ((line == 2) & lane_group(3, 3)) | ((line == 3) & lane_group(0, 0))

    @pl.loop(0, tiles, unroll=8)
    def _(t):
        front = route_ref[0, t]
        back = route_ref[1, t]
        near = got_ref[pl.ds(pl.multiple_of(8 * front, 8), 8), :]
        far = got_ref[pl.ds(pl.multiple_of(8 * jnp.maximum(back, 0), 8), 8), :]
        keep = jnp.where(line >= 6, near, 0.0)
        keep = keep + pltpu.roll(keep, 4, 0)
        keep = keep + pltpu.roll(keep, 2, 0)
        tile = near + jnp.where(back >= 0, keep * far, 0.0)
        out_ref[pl.ds(route_ref[2, t], 6), :] = tile[0:6, :]
        two_up = pltpu.roll(tile, 6, 0)
        edge = jnp.where(from_half, pltpu.roll(pltpu.roll(tile, 4, 0), 64, 1), tile)
        edge = jnp.where(from_left, pltpu.roll(two_up, 16, 1), edge)
        edge = jnp.where(from_right, pltpu.roll(two_up, LANES - 16, 1), edge)
        low = route_ref[3, t]
        high = route_ref[4, t]
        out_ref[pl.ds(low, 1), :] = edge[1:2, :]
        out_ref[pl.ds(low + 1, 1), :] = edge[3:4, :]
        out_ref[pl.ds(high, 1), :] = edge[0:1, :]
        out_ref[pl.ds(high + 1, 1), :] = edge[2:3, :]


def window_taps():
    raw = [math.exp(-k * k / 4.5) for k in range(6)]
    whole = raw[0] + 2.0 * sum(raw[1:])
    return [value / whole for value in raw]


def across_rows(tall, rows, first, count):
    taps = window_taps()
    around = (count + 2) * LANES
    blurred = []
    for f in range(tall.shape[0]):
        given = tall[f, rows, LANES * first : LANES * first + around]
        near = [pltpu.roll(given, 1, 1), given, pltpu.roll(given, around - 1, 1), pltpu.roll(given, around - 2, 1)]
        far = []
        for a in range(3):
            total = None
            for b in range(4):
                if 4 * a + b < 11:
                    term = taps[abs(4 * a + b - 5)] * near[b]
                    total = term if total is None else total + term
            far.append(total)
        total = pltpu.roll(far[0], 4, 1) + far[1] + pltpu.roll(far[2], around - 4, 1)
        blurred.append(total[:, LANES : LANES + count * LANES])
    return blurred


def clear_sides(tall):
    blank = jnp.zeros((tall.shape[0], 16, LANES), F32)
    tall[:, :, 0:LANES] = blank
    tall[:, :, tall.shape[2] - LANES :] = blank


def down_columns(fields, u, f):
    taps = window_taps()
    total = taps[0] * fields[u, f, 8:24, :]
    for k in range(1, 6):
        total = total + taps[k] * (fields[u, f, 8 - k : 24 - k, :] + fields[u, f, 8 + k : 24 + k, :])
    return total


def span(j):
    return pl.ds(pl.multiple_of(LANES * j, LANES), LANES)


RUN = 5
WIDE = 15
HALVES = (slice(0, 16),)


def target_kernel(target_ref, up_ref, down_ref, late_ref, out_ref, fields, tall):
    del late_ref
    spans = target_ref.shape[3] // LANES
    clear_sides(tall)

    @pl.loop(0, 3)
    def _(c):
        @pl.loop(0, spans // RUN)
        def _(run):
            for u in range(RUN):
                j = RUN * run + u
                for low, high, y in (
                    (3, 8, up_ref[c, :, span(j)]),
                    (8, 24, target_ref[0, c, :, span(j)]),
                    (24, 29, down_ref[c, :, span(j)]),
                ):
                    fields[u, 0, low:high, :] = y
                    fields[u, 1, low:high, :] = y * y
            for u in range(RUN):
                for f in range(2):
                    tall[f, :, span(RUN * run + u + 1)] = down_columns(fields, u, f)

        for first in range(0, spans, WIDE):
            count = WIDE
            for rows in HALVES:
                for f, value in enumerate(across_rows(tall, rows, first, count)):
                    out_ref[f, c, rows, LANES * first : LANES * (first + count)] = value


def finish_kernel(
    groups, rcap, per_row,
    code_ref, me_ref, got_ref, target_ref, fixed_ref, target_up, target_down, image_ref, loss_ref,
    board, edges, halo, fields, tall,
):
    cells = got_ref.shape[0]
    spans = target_ref.shape[3] // LANES

    @pl.loop(0, cells)
    def _(cell):
        line = cell * groups + me_ref[2]

        def spot(k):
            column = code_ref[line, k] - 1
            return jnp.where(column < 0, per_row, column)

        for k in range(rcap):
            board[pl.ds(8 * spot(k), 6), :] = got_ref[cell, 6 * k : 6 * k + 6, :]
        for side in range(2):
            for k in range(rcap):
                first = (6 + 2 * side) * rcap + 2 * k
                edges[side, pl.ds(2 * spot((1 + side) * rcap + k), 2), :] = got_ref[cell, first : first + 2, :]

    masks = [jnp.bitwise_and(iota((8, LANES), 1) >> 4, bit) != 0 for bit in (1, 2, 4)]

    def pixels(made):
        made = pltpu.roll(made, 0, 1, stride=16, stride_axis=0)
        for mask, bit in zip(masks, (1, 2, 4)):
            made = jnp.where(mask, pltpu.roll(made, 8 - bit, 0), made)
        return pltpu.roll(made, 0, 1, stride=16, stride_axis=0)

    for j in range(spans):
        lanes = slice(LANES * j, LANES * j + LANES)
        for c in range(3):
            for h in range(2):
                image_ref[0, c, 8 * h : 8 * h + 8, lanes] = pixels(
                    board[pl.ds(64 * j + 2 * c + h, 8, stride=8), :]
                )
        for side in range(2):
            kept = me_ref[3 + side] > 0
            first = edges[side, pl.ds(16 * j, 8, stride=2), :]
            second = edges[side, pl.ds(16 * j + 1, 8, stride=2), :]
            half = pltpu.roll(first, 64, 1)
            left = pltpu.roll(second, LANES - 16, 1)
            right = pltpu.roll(second, 16, 1)
            if side == 0:
                third = jnp.where(lane_group(2, 4), half, jnp.where(lane_group(1, 1), right, left))
            else:
                third = jnp.where(lane_group(5, 7), half, jnp.where(lane_group(4, 4), right, left))
            for c, value in enumerate((first, second, third)):
                halo[side, c, :, lanes] = jnp.where(kept, pixels(value), 0.0)

    clear_sides(tall)

    @pl.loop(0, 3)
    def _(c):
        @pl.loop(0, spans // RUN)
        def _(run):
            for u in range(RUN):
                j = RUN * run + u
                for low, high, x, y in (
                    (3, 8, halo[0, c, 3:8, span(j)], target_up[c, :, span(j)]),
                    (8, 24, image_ref[0, c, :, span(j)], target_ref[0, c, :, span(j)]),
                    (24, 29, halo[1, c, 0:5, span(j)], target_down[c, :, span(j)]),
                ):
                    fields[u, 0, low:high, :] = x
                    fields[u, 1, low:high, :] = x * x
                    fields[u, 2, low:high, :] = x * y
            for u in range(RUN):
                for f in range(3):
                    tall[f, :, span(RUN * run + u + 1)] = down_columns(fields, u, f)

        for first in range(0, spans, WIDE):
            count = WIDE
            lanes = slice(LANES * first, LANES * (first + count))
            for rows in HALVES:
                mx, xx, xy = across_rows(tall, rows, first, count)
                my = fixed_ref[0, c, rows, lanes]
                both = mx * my
                sums = mx * mx + my * my
                ssim = (2.0 * both + 0.0001) * (2.0 * (xy - both) + 0.0009) / (
                    (sums + 0.0001) * (xx + fixed_ref[1, c, rows, lanes] - sums + 0.0009)
                )
                gap = jnp.abs(image_ref[0, c, rows, lanes] - target_ref[0, c, rows, lanes])
                part = (0.8 / 3.0) * gap - (0.2 / 3.0) * ssim
                loss_ref[0, rows, lanes] = jnp.where(c == 0, 0.2, loss_ref[0, rows, lanes]) + part


def call(kernel, outs, specs, scratch=(), mem=8, work=0, out_space=VMEM):
    return pl.pallas_call(
        kernel,
        out_shape=outs,
        in_specs=[pl.BlockSpec(memory_space=spec) for spec in specs],
        out_specs=jax.tree.map(lambda _: pl.BlockSpec(memory_space=out_space), outs),
        scratch_shapes=list(scratch),
        cost_estimate=pl.CostEstimate(flops=work, bytes_accessed=0, transcendentals=0) if work else None,
        compiler_params=pltpu.CompilerParams(vmem_limit_bytes=mem * 2**20),
    )


def local(gauss_params, visible, cameras, tile_ids, tile_blocks, target):
    cells = lax.axis_size("cell")
    groups = lax.axis_size("view")
    devices = cells * groups
    half = cells // 2
    quarter = cells // 4
    blocks = gauss_params.shape[1] // GBLK
    cap = -(-blocks // devices)
    width = target.shape[3]
    per_row = width // 16
    tiles = tile_ids.shape[2]
    rcap = -(-tiles // cells)
    length = tile_blocks.shape[3]
    rows = LANES + 32
    shape = jax.ShapeDtypeStruct
    my_cell = lax.axis_index("cell").astype(jnp.int32)
    my_view = lax.axis_index("view").astype(jnp.int32)
    place = (my_cell + (cells - quarter)) % half
    me = jnp.stack(
        [my_cell * groups + my_view, my_cell, my_view]
        + [(place != edge).astype(jnp.int32) for edge in (0, half - 1)]
    )
    down_pairs = [(s, (s + 1) % cells) for s in range(cells) if (s - quarter) % half != half - 1]
    up_pairs = [(b, a) for a, b in down_pairs]
    lists = jnp.swapaxes(tile_blocks[0, 0], 0, 1)
    own_table = jnp.concatenate([lists, tile_ids[0]], axis=0)
    table = lax.all_to_all(
        jnp.broadcast_to(own_table, (devices, length + 1, tiles)),
        ("cell", "view"), split_axis=0, concat_axis=0, tiled=True,
    )
    work = blocks * GBLK * 10000
    feats = call(
        prepare_kernel,
        shape((visible.shape[0], 9, rows, GBLK), F32),
        [SMEM, HBM, HBM],
        [
            VMEM((512, LANES), F32),
            VMEM((64, LANES), jnp.int32),
            VMEM(gauss_params.shape, F32),
            VMEM(visible.shape, jnp.int32),
            pltpu.SemaphoreType.DMA((PIECES + 1,)),
        ],
        50, work,
    )(cameras, gauss_params, visible)
    edge = shape((3, 5, width), F32)
    made, target_head, target_tail = call(
        functools.partial(render_kernel, cells, groups, cap, per_row, blocks),
        (HBM((devices, 8 * cap, LANES), F32), HBM(edge.shape, F32), HBM(edge.shape, F32)),
        [SMEM, VMEM, VMEM, VMEM],
        [
            VMEM((length + 1, devices, LANES), F32),
            VMEM((2 * LANES, LANES), F32),
            VMEM((2, 9, LANES, LANES), F32),
            VMEM((1024, LANES), F32),
            VMEM((256, LANES), F32),
            VMEM((rows * 8, LANES), F32),
            VMEM((devices, LANES), jnp.int32),
            SMEM((devices, LANES), jnp.int32),
            VMEM((devices, 8 * cap, LANES), F32),
            VMEM((2,) + edge.shape, F32),
            pltpu.SemaphoreType.DMA((4,)),
        ],
        12, work, HBM,
    )(me, table, feats, target)
    target_up = lax.ppermute(target_tail, "cell", down_pairs)
    target_down = lax.ppermute(target_head, "cell", up_pairs)
    got = lax.all_to_all(made, ("cell", "view"), split_axis=0, concat_axis=0, tiled=True)
    planes = shape((1, 3, 16, width), F32)
    route, code = call(
        functools.partial(route_kernel, cells, blocks, cap, rcap, per_row),
        (shape((8, LANES), jnp.int32), shape((devices, LANES), jnp.int32)),
        [SMEM, VMEM, pl.ANY],
        [VMEM((LANES, LANES), F32), VMEM((devices, LANES), F32)],
        8, work,
    )(me, table, target_head)
    tile_rows = call(
        functools.partial(combine_kernel, tiles),
        shape((cells * 10 * rcap, LANES), F32),
        [SMEM, VMEM, pl.ANY, pl.ANY],
    )(route, got.reshape(devices * cap * 8, LANES), target_up, target_down)
    got_tiles = lax.all_to_all(
        tile_rows.reshape(cells, 10 * rcap, LANES), "cell", split_axis=0, concat_axis=0, tiled=True
    )
    fixed = call(
        target_kernel,
        shape((2, 3, 16, width), F32),
        [VMEM] * 3 + [pl.ANY],
        [VMEM((RUN, 2, 32, LANES), F32), VMEM((2, 16, width + 2 * LANES), F32)],
        8, work,
    )(target, target_up, target_down, tile_rows)
    return call(
        functools.partial(finish_kernel, groups, rcap, per_row),
        (planes, shape((1, 16, width), F32)),
        [SMEM, SMEM] + [VMEM] * 5,
        [
            VMEM((8 * (per_row + 1), LANES), F32),
            VMEM((2, 2 * (per_row + 4), LANES), F32),
            VMEM((2, 3, 8, width), F32),
            VMEM((RUN, 3, 32, LANES), F32),
            VMEM((3, 16, width + 2 * LANES), F32),
        ],
        8,
    )(code, me, got_tiles, target, fixed, target_up, target_down)


def solution(mesh):
    return jax.shard_map(
        local,
        mesh=mesh,
        in_specs=(
            P(None, ("cell", "view")),
            P(None, ("cell", "view")),
            P(),
            P("cell", "view", None),
            P("cell", "view", None, None),
            P("view", None, "cell", None),
        ),
        out_specs=(P("view", None, "cell", None), P("view", "cell", None)),
        check_vma=False,
    )
```
